32 devices in a mesh: gx: 8 (over y, x, core), gy: 4 (over z).
Axes of the slice: x: 2, y: 2, z: 4, core: 2. Of those that a mesh axis runs over, the one named last changes fastest.
Arguments:
- velocity: float32 [3, 128, 64, 512], P(None, 'gx', 'gy'), may hold values from -6 to 6
- stress: float32 [6, 128, 64, 512], P(None, 'gx', 'gy'), may hold values from -6 to 6
- pier_velocity: float32 [128, 16], P('gx', 'gy'), may hold values from -6 to 6
- buoyancy: float32 [128, 64, 512], P('gx', 'gy'), may hold values from 0.5 to 2
- layer: int32 [128], P('gx'), may hold values from 0 to 7, as said below
- lame_table: float32 [8], replicated, may hold values from 0.3 to 1.2
- shear_table: float32 [8], replicated, may hold values from 0.2 to 0.8
- relax_table: float32 [8], replicated, may hold values from 0.6 to 0.95
- impedance: float32 [16], P('gy'), may hold values from 0.5 to 2
- footprint: int32 [16, 16], replicated, may hold values from 0 to 32767, as said below
- damp_inverse: float32 [128, 128], replicated
Outputs:
- velocity_out: float32 [3, 128, 64, 512], P(None, 'gx', 'gy')
- stress_out: float32 [6, 128, 64, 512], P(None, 'gx', 'gy')
- pier_out: float32 [128, 16], P('gx', 'gy')
The draws below stay inside these ranges and needn't reach their ends.
Inputs may be any that keep to these rules, and one draw needn't show every extreme that they name: `footprint`: row p lists the 16 cells of a square of 4 by 4 cells, row by row; squares may intersect and lie anywhere in the plane. `layer`: non-decreasing along depth; the first cell is in layer 0 and the last in layer 7.
All inputs are finite; a program needn't handle non-finite values.
Results may differ from the reference program's by a relative error of at most 0.00011.
Values sent between devices are 32-bit elements; how exact they have to be, the bound alone decides.
A program may use at most 192 MiB of HBM per device.

```python
import math
import jax
import jax.numpy as jnp
from jax import lax

NX = 512
FOOT_SIDE = 4
NLAYER = 8
STEPS = 2
NZ = 128
NY = 64
NPIER = 16
FOOT = 16


def draw_damp_inverse(key, part):
    key_diag, key_off = jax.random.split(jax.random.fold_in(key, 7))
    diagonal = jax.random.uniform(key_diag, (NZ,), jnp.float32, 0.6, 1.0)
    spread = jax.random.normal(key_off, (NZ, NZ), jnp.float32) * (0.5 / math.sqrt(NZ))
    return jnp.eye(NZ, dtype=jnp.float32) * diagonal[:, None] + spread


def draw_footprint(key, part):
    key_rows, key_cols, key_high, key_low = jax.random.split(jax.random.fold_in(key, 11), 4)
    rows = jax.random.randint(key_rows, (NPIER,), 0, NY - FOOT_SIDE + 1)
    cols = jax.random.randint(key_cols, (NPIER,), 0, NX - FOOT_SIDE + 1)
    high = jax.random.randint(key_high, (), 0, NPIER)
    low = (high + 1 + jax.random.randint(key_low, (), 0, NPIER - 1)) % NPIER
    pier_ids = jnp.arange(NPIER, dtype=jnp.int32)
    rows = jnp.where(pier_ids == high, NY - FOOT_SIDE, rows)
    rows = jnp.where(pier_ids == low, 0, rows)
    cols = jnp.where(pier_ids == high, NX - FOOT_SIDE, cols)
    cols = jnp.where(pier_ids == low, 0, cols)
    offsets = jnp.arange(FOOT, dtype=jnp.int32)
    cells = (rows[:, None] + offsets[None, :] // FOOT_SIDE) * NX + cols[:, None] + offsets[None, :] % FOOT_SIDE
    return cells.astype(jnp.int32)


def draw_layer(key, part):
    depth_ids = jnp.arange(NZ, dtype=jnp.int32)
    rises = (jax.random.randint(jax.random.fold_in(key, 23), (NZ,), 0, NZ) < NLAYER).astype(jnp.int32)
    rises = jnp.where(depth_ids == 0, 0, rises)
    levels = jnp.minimum(jnp.cumsum(rises), NLAYER - 1)
    return jnp.where(depth_ids == NZ - 1, NLAYER - 1, levels).astype(jnp.int32)


def level_of(key, extent, shards, least, high):
    gain = 1.0
    for dim, parts in shards:
        steps = jax.random.uniform(jax.random.fold_in(jax.random.fold_in(key, 6), dim), (parts,), jnp.float32, least / len(shards), high / len(shards))
        gain = gain * jnp.repeat(jnp.exp(steps), extent[dim] // parts).reshape((-1,) + (1,) * (len(extent) - 1 - dim))
    return gain


def centred(stream_key, dims, scale, reach, cuts=(), held_as=jnp.bfloat16):
    drawn = scale * jax.random.normal(stream_key, dims, jnp.float32)
    if cuts:
        drawn = drawn * level_of(stream_key, dims, cuts, -0.22, 0.18)
    return jnp.clip(drawn, -reach, reach).astype(held_as)


def setup_inputs(seed: int = 0) -> dict:
    keys = jax.random.split(jax.random.key(seed), 12)
    velocity = centred(keys[0], (3, NZ, NY, NX), 1.0, 6.0, ((1, 8), (2, 4)), jnp.float32)
    stress = centred(keys[1], (6, NZ, NY, NX), 1.0, 6.0, ((1, 8), (2, 4)), jnp.float32)
    pier_velocity = centred(keys[2], (NZ, NPIER), 1.0, 6.0, ((0, 8), (1, 4)), jnp.float32)
    buoyancy = jnp.clip(jnp.exp(math.log(2.0) - 1.3862944 * jax.random.uniform(keys[3], (NZ, NY, NX), jnp.float32) ** level_of(keys[3], (NZ, NY, NX), ((0, 8), (1, 4)), -0.2, 0.2)), 0.5, 2.0)
    layer = draw_layer(jax.random.fold_in(keys[11], 71), 0)
    lame_table = jnp.clip(jnp.exp(jax.random.uniform(keys[5], (NLAYER,), jnp.float32, math.log(0.3), math.log(1.2))), 0.3, 1.2)
    shear_table = jnp.clip(jnp.exp(jax.random.uniform(keys[6], (NLAYER,), jnp.float32, math.log(0.2), math.log(0.8))), 0.2, 0.8)
    relax_table = jnp.clip(jax.random.uniform(keys[7], (NLAYER,), jnp.float32, 0.6, 0.95), 0.6, 0.95)
    impedance = jnp.clip(jnp.exp(math.log(2.0) - 1.3862944 * jax.random.uniform(keys[8], (NPIER,), jnp.float32) ** level_of(keys[8], (NPIER,), ((0, 4),), -0.2, 0.2)), 0.5, 2.0)
    footprint = draw_footprint(jax.random.fold_in(keys[11], 71), 0)
    damp_inverse = draw_damp_inverse(jax.random.fold_in(keys[11], 71), 0)
    return {"velocity": velocity, "stress": stress, "pier_velocity": pier_velocity, "buoyancy": buoyancy, "layer": layer, "lame_table": lame_table, "shear_table": shear_table, "relax_table": relax_table, "impedance": impedance, "footprint": footprint, "damp_inverse": damp_inverse}


grid_ratio = 0.25
soil_gain = 0.2
pier_gain = 0.5


def forward_diff(padded, along):
    center = padded[1:-1, 1:-1, 1:-1]
    if along == 0:
        return padded[2:, 1:-1, 1:-1] - center
    if along == 1:
        return padded[1:-1, 2:, 1:-1] - center
    return padded[1:-1, 1:-1, 2:] - center


def backward_diff(padded, along):
    center = padded[1:-1, 1:-1, 1:-1]
    if along == 0:
        return center - padded[:-2, 1:-1, 1:-1]
    if along == 1:
        return center - padded[1:-1, :-2, 1:-1]
    return center - padded[1:-1, 1:-1, :-2]


def move_velocity(velocity, padded, buoyancy):
    scaled = grid_ratio * buoyancy
    first = velocity[0] + scaled * (backward_diff(padded[0], 2) + forward_diff(padded[3], 1) + forward_diff(padded[4], 0))
    second = velocity[1] + scaled * (forward_diff(padded[3], 2) + backward_diff(padded[1], 1) + forward_diff(padded[5], 0))
    third = velocity[2] + scaled * (forward_diff(padded[4], 2) + forward_diff(padded[5], 1) + backward_diff(padded[2], 0))
    return jnp.stack([first, second, third])


def move_stress(stress, padded, lame_first, shear_mod, relax):
    strain_x = forward_diff(padded[0], 2)
    strain_y = forward_diff(padded[1], 1)
    strain_z = forward_diff(padded[2], 0)
    modulus = lame_first + 2.0 * shear_mod
    normal_x = relax * stress[0] + grid_ratio * (modulus * strain_x + lame_first * (strain_y + strain_z))
    normal_y = relax * stress[1] + grid_ratio * (modulus * strain_y + lame_first * (strain_x + strain_z))
    normal_z = relax * stress[2] + grid_ratio * (modulus * strain_z + lame_first * (strain_x + strain_y))
    shear_xy = relax * stress[3] + grid_ratio * shear_mod * (backward_diff(padded[0], 1) + backward_diff(padded[1], 2))
    shear_xz = relax * stress[4] + grid_ratio * shear_mod * (backward_diff(padded[0], 0) + backward_diff(padded[2], 2))
    shear_yz = relax * stress[5] + grid_ratio * shear_mod * (backward_diff(padded[1], 0) + backward_diff(padded[2], 1))
    return jnp.stack([normal_x, normal_y, normal_z, shear_xy, shear_xz, shear_yz])


def layer_values(layer, table):
    levels = jnp.arange(table.shape[0], dtype=jnp.int32)
    onehot = (layer[:, None] == levels[None, :]).astype(table.dtype)
    return jnp.sum(onehot * table[None, :], axis=1)[:, None, None]


def reference(velocity, stress, pier_velocity, buoyancy, layer, lame_table, shear_table, relax_table, impedance, footprint, damp_inverse):
    lame_first = layer_values(layer, lame_table)
    shear_mod = layer_values(layer, shear_table)
    relax = layer_values(layer, relax_table)
    cells = footprint.reshape(-1)
    for time_step in range(STEPS):
        padded = jnp.pad(stress, ((0, 0), (1, 1), (1, 1), (1, 1)))
        velocity = move_velocity(velocity, padded, buoyancy)
        vertical = velocity[2].reshape(NZ, NY * NX)
        mean_speed = jnp.sum(vertical[:, cells].reshape(NZ, NPIER, FOOT), axis=2) / FOOT
        force = impedance[None, :] * (pier_velocity - mean_speed)
        pier_velocity = pier_velocity - pier_gain * force
        vertical = vertical.at[:, cells].add(soil_gain * jnp.repeat(force, FOOT, axis=1))
        velocity = jnp.stack([velocity[0], velocity[1], vertical.reshape(NZ, NY, NX)])
        flat = velocity.reshape(3, NZ, NY * NX)
        velocity = jnp.einsum("zk,fkm->fzm", damp_inverse, flat, precision=lax.Precision.HIGHEST).reshape(3, NZ, NY, NX)
        padded = jnp.pad(velocity, ((0, 0), (1, 1), (1, 1), (1, 1)))
        stress = move_stress(stress, padded, lame_first, shear_mod, relax)
    return (velocity, stress, pier_velocity)
```

```python
import functools
import jax
import jax.numpy as jnp
from jax import lax
from jax.experimental import pallas as pl
from jax.experimental.pallas import tpu as pltpu
from jax.sharding import PartitionSpec as P

STEPS = 2
FOOT = 16


grid_ratio = 0.25
soil_gain = 0.2
pier_gain = 0.5


def extended(cells, sides, width):
    for axis, dim in sides:
        count = lax.axis_size(axis)
        ends = count - 1
        head = lax.slice_in_dim(cells, 0, width, axis=dim)
        tail = lax.slice_in_dim(cells, cells.shape[dim] - width, cells.shape[dim], axis=dim)
        cells = jnp.concatenate(
            [
                lax.ppermute(tail, axis, [(i, (i + 1) % count) for i in range(ends)]),
                cells,
                lax.ppermute(head, axis, [((i + 1) % count, i) for i in range(ends)]),
            ],
            axis=dim,
        )
    return cells


def forward_diff(padded, along):
    center = padded[1:-1, 1:-1, 1:-1]
    if along == 0:
        return padded[2:, 1:-1, 1:-1] - center
    if along == 1:
        return padded[1:-1, 2:, 1:-1] - center
    return padded[1:-1, 1:-1, 2:] - center


def backward_diff(padded, along):
    center = padded[1:-1, 1:-1, 1:-1]
    if along == 0:
        return center - padded[:-2, 1:-1, 1:-1]
    if along == 1:
        return center - padded[1:-1, :-2, 1:-1]
    return center - padded[1:-1, 1:-1, :-2]


def move_velocity(velocity, padded, buoyancy):
    scaled = grid_ratio * buoyancy
    first = velocity[0] + scaled * (
        backward_diff(padded[0], 2) + forward_diff(padded[3], 1) + forward_diff(padded[4], 0)
    )
    second = velocity[1] + scaled * (
        forward_diff(padded[3], 2) + backward_diff(padded[1], 1) + forward_diff(padded[5], 0)
    )
    third = velocity[2] + scaled * (
        forward_diff(padded[4], 2) + forward_diff(padded[5], 1) + backward_diff(padded[2], 0)
    )
    return jnp.stack([first, second, third])


def move_stress(stress, padded, lame_first, shear_mod, relax):
    strain_x = forward_diff(padded[0], 2)
    strain_y = forward_diff(padded[1], 1)
    strain_z = forward_diff(padded[2], 0)
    modulus = lame_first + 2.0 * shear_mod
    normal_x = relax * stress[0] + grid_ratio * (
        modulus * strain_x + lame_first * (strain_y + strain_z)
    )
    normal_y = relax * stress[1] + grid_ratio * (
        modulus * strain_y + lame_first * (strain_x + strain_z)
    )
    normal_z = relax * stress[2] + grid_ratio * (
        modulus * strain_z + lame_first * (strain_x + strain_y)
    )
    shear_xy = relax * stress[3] + grid_ratio * shear_mod * (
        backward_diff(padded[0], 1) + backward_diff(padded[1], 2)
    )
    shear_xz = relax * stress[4] + grid_ratio * shear_mod * (
        backward_diff(padded[0], 0) + backward_diff(padded[2], 2)
    )
    shear_yz = relax * stress[5] + grid_ratio * shear_mod * (
        backward_diff(padded[1], 0) + backward_diff(padded[2], 1)
    )
    return jnp.stack([normal_x, normal_y, normal_z, shear_xy, shear_xz, shear_yz])


def layer_values(layer, table):
    levels = jnp.arange(table.shape[0], dtype=jnp.int32)
    onehot = (layer[:, None] == levels[None, :]).astype(table.dtype)
    return jnp.sum(onehot * table[None, :], axis=1)[:, None, None]


def with_faces(fields):
    padded = extended(fields, (("gx", 1), ("gy", 2)), 1)
    return jnp.pad(padded, ((0, 0), (0, 0), (0, 0), (1, 1)))


def footprint_matches(cell_ids, footprint):
    piers = footprint.shape[0]
    equal = (cell_ids[:, None] == footprint.reshape(-1)[None, :]).astype(jnp.float32)
    return jnp.sum(equal.reshape(cell_ids.shape[0], piers, FOOT), axis=2)


def damp_columns(velocity, inverse):
    pencils = lax.all_to_all(velocity, "gx", split_axis=3, concat_axis=1, tiled=True)
    shape = pencils.shape
    flat = pencils.reshape(shape[0], shape[1], shape[2] * shape[3])
    damped = jnp.einsum("zk,fkm->fzm", inverse, flat, precision=lax.Precision.HIGHEST).reshape(
        shape
    )
    return lax.all_to_all(damped, "gx", split_axis=1, concat_axis=3, tiled=True)


def body(
    velocity,
    stress,
    pier_velocity,
    buoyancy,
    layer,
    lame_table,
    shear_table,
    relax_table,
    impedance,
    footprint,
    damp_inverse,
):
    depth_cells, side_cells, line_cells = (velocity.shape[1], velocity.shape[2], velocity.shape[3])
    own_piers = pier_velocity.shape[1]
    lame_first = layer_values(layer, lame_table)
    shear_mod = layer_values(layer, shear_table)
    relax = layer_values(layer, relax_table)
    row_start = lax.axis_index("gy") * side_cells
    cell_ids = row_start * line_cells + jnp.arange(side_cells * line_cells, dtype=jnp.int32)
    selector = footprint_matches(cell_ids, footprint)
    own_foot = lax.dynamic_slice_in_dim(footprint, lax.axis_index("gy") * own_piers, own_piers, 0)
    for time_step in range(STEPS):
        padded = with_faces(stress)
        velocity = move_velocity(velocity, padded, buoyancy)
        vertical = velocity[2].reshape(depth_cells, side_cells * line_cells)
        piece = lax.all_gather(velocity[2], "gy", axis=1, tiled=True)
        count = piece.shape[1]
        piece_ids = jnp.arange(count * line_cells, dtype=jnp.int32)
        picks = footprint_matches(piece_ids, own_foot)
        flat = piece.reshape(depth_cells, count * line_cells)
        summed = jnp.dot(
            flat, picks, precision=lax.Precision.HIGHEST, preferred_element_type=jnp.float32
        )
        mean_speed = summed / FOOT
        force = impedance[None, :] * (pier_velocity - mean_speed)
        pier_velocity = pier_velocity - pier_gain * force
        all_force = lax.all_gather(force, "gy", axis=1, tiled=True)
        pushed = jnp.dot(
            all_force,
            selector.T,
            precision=lax.Precision.HIGHEST,
            preferred_element_type=jnp.float32,
        )
        vertical = vertical + soil_gain * pushed
        velocity = jnp.stack(
            [velocity[0], velocity[1], vertical.reshape(depth_cells, side_cells, line_cells)]
        )
        velocity = damp_columns(velocity, damp_inverse)
        padded = with_faces(velocity)
        stress = move_stress(stress, padded, lame_first, shear_mod, relax)
    return (velocity, stress, pier_velocity)


SIDE = 4
LANES = 128
ROWS = 8
MESH = pl.DeviceIdType.MESH
Z_GHOSTS = ((2, -1), (4, 1), (5, 1))
Y_GHOSTS = ((1, -1), (3, 1), (5, 1))


def shift_x(a, ahead):
    lane = lax.broadcasted_iota(jnp.int32, a.shape, 1)
    width = a.shape[1]
    if ahead:
        return jnp.where(lane == width - 1, 0.0, pltpu.roll(a, width - 1, 1))
    return jnp.where(lane == 0, 0.0, pltpu.roll(a, 1, 1))


def fused(
    n, ng, v_hbm, s_hbm, b_hbm, coef_hbm, w_ref, imp_ref, row_ref, col_ref, damp_ref,
    v_out, s_out, w_out,
    v_ext, s_ext, buoy, coef, acc, pin, pout, um, wbuf, sg_send, sg_recv, yg_send, yg_recv,
    load_sem, zs_send, zs_recv, cf_send, cf_recv, ys_send, ys_recv,
    f_send, f_recv, r_send, r_recv, u_send, u_recv, y_send, y_recv, o_sem,
):
    me = lax.axis_index("gx")
    g = lax.axis_index("gy")
    depth, side, line = buoy.shape
    tiles = line // LANES
    inner = pl.ds(ROWS, side)

    def piece(j):
        return (
            pl.ds(pl.multiple_of((j // tiles) * ROWS, ROWS), ROWS),
            pl.ds(pl.multiple_of((j % tiles) * LANES, LANES), LANES),
        )

    loads = {}
    for slot, f in enumerate((1, 3, 5, 2, 4, 0)):
        loads[("s", f)] = pltpu.make_async_copy(
            s_hbm.at[f], s_ext.at[f, pl.ds(1, depth), inner, :], load_sem.at[slot]
        )
    loads["b"] = pltpu.make_async_copy(b_hbm, buoy, load_sem.at[6])
    for f in range(3):
        loads[("v", f)] = pltpu.make_async_copy(
            v_hbm.at[f], v_ext.at[f, pl.ds(1, depth), inner, :], load_sem.at[7 + f]
        )
    loads["c"] = pltpu.make_async_copy(coef_hbm, coef.at[:, pl.ds(1, depth)], load_sem.at[10])
    for copy in loads.values():
        copy.start()

    plane = jnp.zeros((side, line), jnp.float32)
    for f, way in Z_GHOSTS:
        s_ext[f, 0 if way < 0 else depth + 1, inner, :] = plane
    edge = jnp.zeros((ROWS, line), jnp.float32)

    def clear(k, carry):
        for f, way in Y_GHOSTS:
            s_ext[f, k, pl.ds(0 if way < 0 else ROWS + side, ROWS), :] = edge
        for f in range(3):
            v_ext[f, k, pl.ds(0, ROWS), :] = edge
            v_ext[f, k, pl.ds(ROWS + side, ROWS), :] = edge
        return carry

    lax.fori_loop(0, depth + 2, clear, 0)
    for c in range(3):
        coef[c, 0] = jnp.zeros((ROWS, LANES), jnp.float32)
        coef[c, depth + 1] = jnp.zeros((ROWS, LANES), jnp.float32)
        pout[c, 0] = jnp.zeros((ROWS, LANES), jnp.float32)
        pout[c, n * depth + 1] = jnp.zeros((ROWS, LANES), jnp.float32)

    barrier = pltpu.get_barrier_semaphore()
    for d in range(1, n):
        pl.semaphore_signal(
            barrier, inc=1, device_id=(lax.rem(me + d, n), g), device_id_type=MESH
        )
    for d in range(1, ng):
        pl.semaphore_signal(
            barrier, inc=1, device_id=(me, lax.rem(g + d, ng)), device_id_type=MESH
        )
    pl.semaphore_wait(barrier, n - 1 + ng - 1)

    def z_copy(i):
        f, way = Z_GHOSTS[i]
        return pltpu.make_async_remote_copy(
            src_ref=s_hbm.at[f, depth - 1 if way < 0 else 0],
            dst_ref=s_ext.at[f, 0 if way < 0 else depth + 1, inner, :],
            send_sem=zs_send.at[i],
            recv_sem=zs_recv.at[i],
            device_id=(me - way, g),
            device_id_type=MESH,
        )

    def c_copy(way):
        i = (way + 1) // 2
        return pltpu.make_async_remote_copy(
            src_ref=coef_hbm.at[:, depth - 1 if way < 0 else 0],
            dst_ref=coef.at[:, 0 if way < 0 else depth + 1],
            send_sem=cf_send.at[i],
            recv_sem=cf_recv.at[i],
            device_id=(me - way, g),
            device_id_type=MESH,
        )

    def y_stress(i):
        f, way = Y_GHOSTS[i]
        return pltpu.make_async_remote_copy(
            src_ref=sg_send.at[i],
            dst_ref=sg_recv.at[i],
            send_sem=ys_send.at[i],
            recv_sem=ys_recv.at[i],
            device_id=(me, g - way),
            device_id_type=MESH,
        )

    not_ends = {
        -1: (me > 0, me < n - 1, g > 0, g < ng - 1),
        1: (me < n - 1, me > 0, g < ng - 1, g > 0),
    }

    for i, (f, way) in enumerate(Z_GHOSTS):
        @pl.when(not_ends[way][1])
        def _(i=i):
            z_copy(i).start()
    for way in (-1, 1):
        @pl.when(not_ends[way][1])
        def _(way=way):
            c_copy(way).start()
    for i, (f, way) in enumerate(Y_GHOSTS):
        loads[("s", f)].wait()
        sg_send[i] = s_ext[f, pl.ds(1, depth), ROWS + side - 1 if way < 0 else ROWS, :]

        @pl.when(not_ends[way][3])
        def _(i=i):
            y_stress(i).start()
    for key, copy in loads.items():
        if key not in (("s", 1), ("s", 3), ("s", 5)):
            copy.wait()

    ids = lax.broadcasted_iota(jnp.int32, (side, LANES), 0) + g * side
    first = row_ref[0:1, :]
    in_rows = jnp.where((ids >= first) & (ids < first + SIDE), 1.0, 0.0)
    across = lax.broadcasted_iota(jnp.int32, (LANES, line), 1)
    start = jnp.concatenate([col_ref[...]] * tiles, axis=1)
    in_cols = jnp.where((across >= start) & (across < start + SIDE), 1.0, 0.0)

    for i, (f, way) in enumerate(Z_GHOSTS):
        @pl.when(not_ends[way][0])
        def _(i=i):
            z_copy(i).wait_recv()

        @pl.when(not_ends[way][1])
        def _(i=i):
            z_copy(i).wait_send()
    for way in (-1, 1):
        @pl.when(not_ends[way][0])
        def _(way=way):
            c_copy(way).wait_recv()

        @pl.when(not_ends[way][1])
        def _(way=way):
            c_copy(way).wait_send()
    for i, (f, way) in enumerate(Y_GHOSTS):
        @pl.when(not_ends[way][2])
        def _(i=i, f=f, way=way):
            y_stress(i).wait_recv()
            s_ext[f, pl.ds(1, depth), ROWS - 1 if way < 0 else ROWS + side, :] = sg_recv[i]

        @pl.when(not_ends[way][3])
        def _(i=i):
            y_stress(i).wait_send()

    def cells(ref, f, k, shift=0, begin=ROWS, rows=None):
        return ref[f, k, pl.ds(begin + shift, side if rows is None else rows), :]

    def speed_x(i, carry):
        k = i + 1
        xx, xy, xz = cells(s_ext, 0, k), cells(s_ext, 3, k), cells(s_ext, 4, k)
        total = (xx - shift_x(xx, False)) + (cells(s_ext, 3, k, 1) - xy)
        total = total + (cells(s_ext, 4, k + 1) - xz)
        acc[0, i] = cells(v_ext, 0, k) + (grid_ratio * buoy[i]) * total
        return carry

    def speed_y(i, carry):
        k = i + 1
        xy, yy, yz = cells(s_ext, 3, k), cells(s_ext, 1, k), cells(s_ext, 5, k)
        total = (shift_x(xy, True) - xy) + (yy - cells(s_ext, 1, k, -1))
        total = total + (cells(s_ext, 5, k + 1) - yz)
        acc[1, i] = cells(v_ext, 1, k) + (grid_ratio * buoy[i]) * total
        return carry

    def speed_z(i, carry):
        k = i + 1
        xz, yz, zz = cells(s_ext, 4, k), cells(s_ext, 5, k), cells(s_ext, 2, k)
        total = (shift_x(xz, True) - xz) + (cells(s_ext, 5, k, 1) - yz)
        total = total + (zz - cells(s_ext, 2, k - 1))
        acc[2, i] = cells(v_ext, 2, k) + (grid_ratio * buoy[i]) * total
        return carry

    def wide(c, k, rows):
        tile = jnp.concatenate([coef[c, k]] * tiles, axis=1)
        return jnp.concatenate([tile] * (rows // ROWS), axis=0)

    def normals(k, begin, rows):
        at = functools.partial(cells, begin=begin, rows=rows)
        lame, shear, relax = (wide(c, k, rows) for c in range(3))
        vx, vy, vz = at(v_ext, 0, k), at(v_ext, 1, k), at(v_ext, 2, k)
        ex = shift_x(vx, True) - vx
        ey = at(v_ext, 1, k, 1) - vy
        ez = at(v_ext, 2, k + 1) - vz
        modulus = lame + 2.0 * shear
        for f, own, others in ((0, ex, ey + ez), (1, ey, ex + ez), (2, ez, ex + ey)):
            s_ext[f, k, pl.ds(begin, rows), :] = relax * at(s_ext, f, k) + grid_ratio * (
                modulus * own + lame * others
            )

    def shears(k, begin, rows):
        at = functools.partial(cells, begin=begin, rows=rows)
        shear, relax = wide(1, k, rows), wide(2, k, rows)
        shear = grid_ratio * shear
        vx, vy, vz = at(v_ext, 0, k), at(v_ext, 1, k), at(v_ext, 2, k)
        xy = (vx - at(v_ext, 0, k, -1)) + (vy - shift_x(vy, False))
        xz = (vx - at(v_ext, 0, k - 1)) + (vz - shift_x(vz, False))
        yz = (vy - at(v_ext, 1, k - 1)) + (vz - at(v_ext, 2, k, -1))
        for f, strain in ((3, xy), (4, xz), (5, yz)):
            s_ext[f, k, pl.ds(begin, rows), :] = relax * at(s_ext, f, k) + shear * strain

    def there(step, f, d):
        t = lax.rem(me + d, n)
        ys, xs = piece(t)
        src = acc.at[f, :, ys, xs]
        dst = pin.at[f, pl.ds(me * depth, depth)]
        if d == 0:
            return pltpu.make_async_copy(src, dst, f_recv.at[step, f, 0])
        return pltpu.make_async_remote_copy(
            src_ref=src, dst_ref=dst, send_sem=f_send.at[step, f, d],
            recv_sem=f_recv.at[step, f, d], device_id=(t, g), device_id_type=MESH,
        )

    def back(step, f, d):
        t = lax.rem(me + d, n)
        ys, xs = pl.ds(pl.multiple_of((me // tiles) * ROWS + ROWS, ROWS), ROWS), piece(me)[1]
        src = pout.at[f, pl.ds(t * depth, depth + 2)]
        dst = v_ext.at[f, :, ys, xs]
        if d == 0:
            return pltpu.make_async_copy(src, dst, r_recv.at[step, f, 0])
        return pltpu.make_async_remote_copy(
            src_ref=src, dst_ref=dst, send_sem=r_send.at[step, f, d],
            recv_sem=r_recv.at[step, f, d], device_id=(t, g), device_id_type=MESH,
        )

    def start_all(make, step, f):
        for d in list(range(1, n)) + [0]:
            make(step, f, d).start()

    def wait_sent(make, step, f):
        for d in range(1, n):
            make(step, f, d).wait_send()

    def wait_got(make, step, f):
        make(step, f, 0).wait()
        for d in range(1, n):
            make(step, f, d).wait_recv()

    def share(step, d):
        return pltpu.make_async_remote_copy(
            src_ref=um.at[step, 0], dst_ref=um.at[step, d],
            send_sem=u_send.at[step, d], recv_sem=u_recv.at[step, d],
            device_id=(me, lax.rem(g + d, ng)), device_id_type=MESH,
        )

    def y_speed(step, f, i):
        return pltpu.make_async_remote_copy(
            src_ref=yg_send.at[step, f, i], dst_ref=yg_recv.at[step, f, i],
            send_sem=y_send.at[step, f, i], recv_sem=y_recv.at[step, f, i],
            device_id=(me, g + 1 - 2 * i), device_id_type=MESH,
        )

    has_next, has_last = g < ng - 1, g > 0
    planes = pl.ds(0, depth + 2)

    for step in range(STEPS):
        if step > 0:
            for f in range(3):
                wait_sent(there, step - 1, f)
        lax.fori_loop(0, depth, speed_z, 0)
        flat = acc[2].reshape(depth * side, line)
        part = lax.dot_general(
            flat, in_cols, (((1,), (1,)), ((), ())),
            precision=lax.Precision.HIGHEST, preferred_element_type=jnp.float32,
        ).reshape(depth, side, LANES)
        um[step, 0, pl.ds(0, depth), :] = jnp.sum(part * in_rows[None], axis=1)
        um[step, 0, pl.ds(depth, depth), :] = w_ref[...]
        um[step, 0, pl.ds(2 * depth, ROWS), :] = imp_ref[...]
        for d in range(1, ng):
            share(step, d).start()
        lax.fori_loop(0, depth, speed_x, 0)
        start_all(there, step, 0)
        lax.fori_loop(0, depth, speed_y, 0)
        start_all(there, step, 1)
        for d in range(1, ng):
            share(step, d).wait()
        every = um[step, 0]
        for d in range(1, ng):
            every = every + um[step, d]
        w = every[depth : 2 * depth] if step == 0 else wbuf[...]
        force = every[2 * depth : 2 * depth + 1] * (w - every[0:depth] / FOOT)
        wbuf[...] = w - pier_gain * force
        spread = (force[:, None, :] * in_rows[None]).reshape(depth * side, LANES)
        pushed = jnp.dot(
            spread, in_cols, precision=lax.Precision.HIGHEST, preferred_element_type=jnp.float32
        )
        acc[2] = acc[2] + soil_gain * pushed.reshape(depth, side, line)
        start_all(there, step, 2)

        for f in range(3):
            wait_got(there, step, f)
            if step > 0:
                wait_sent(back, step - 1, f)
            full = jnp.concatenate([pin[f, :, y, :] for y in range(ROWS)], axis=1)
            damped = jnp.dot(
                damp_ref[...], full, precision=lax.Precision.HIGHEST,
                preferred_element_type=jnp.float32,
            )
            for y in range(ROWS):
                pout[f, pl.ds(1, n * depth), y, :] = damped[:, y * LANES : (y + 1) * LANES]
            start_all(back, step, f)
        for f in range(3):
            wait_got(back, step, f)
            yg_send[step, f, 0] = v_ext[f, planes, ROWS + side - 1, :]
            yg_send[step, f, 1] = v_ext[f, planes, ROWS, :]

            @pl.when(has_next)
            def _(f=f):
                y_speed(step, f, 0).start()

            @pl.when(has_last)
            def _(f=f):
                y_speed(step, f, 1).start()
            if step == STEPS - 1:
                pltpu.make_async_copy(
                    v_ext.at[f, pl.ds(1, depth), inner, :], v_out.at[f], o_sem.at[f]
                ).start()
        if step == STEPS - 1:
            for f in range(3):
                pltpu.make_async_copy(
                    v_ext.at[f, pl.ds(1, depth), inner, :], v_out.at[f], o_sem.at[f]
                ).wait()
        for f in range(3):
            @pl.when(has_last)
            def _(f=f):
                y_speed(step, f, 0).wait_recv()
                v_ext[f, planes, ROWS - 1, :] = yg_recv[step, f, 0]
                y_speed(step, f, 1).wait_send()

            @pl.when(has_next)
            def _(f=f):
                y_speed(step, f, 1).wait_recv()
                v_ext[f, planes, ROWS + side, :] = yg_recv[step, f, 1]
                y_speed(step, f, 0).wait_send()

        if step < STEPS - 1:
            def stress_wide(i, carry):
                normals(i, 0, ROWS + side)
                shears(i + 1, ROWS, ROWS + side)
                return carry

            lax.fori_loop(0, depth + 1, stress_wide, 0)

            @pl.when(g == 0)
            def _():
                s_ext[1, planes, ROWS - 1, :] = jnp.zeros((depth + 2, line), jnp.float32)

            @pl.when(g == ng - 1)
            def _():
                s_ext[3, planes, ROWS + side, :] = jnp.zeros((depth + 2, line), jnp.float32)
                s_ext[5, planes, ROWS + side, :] = jnp.zeros((depth + 2, line), jnp.float32)
        else:
            def stress_last(i, carry):
                normals(i + 1, ROWS, side)
                shears(i + 1, ROWS, side)
                return carry

            lax.fori_loop(0, depth, stress_last, 0)

    outs = [
        pltpu.make_async_copy(
            s_ext.at[f, pl.ds(1, depth), inner, :], s_out.at[f], o_sem.at[3 + f]
        )
        for f in range(6)
    ]
    for copy in outs:
        copy.start()
    w_out[...] = wbuf[...]
    for f in range(3):
        wait_sent(there, STEPS - 1, f)
        wait_sent(back, STEPS - 1, f)
    for copy in outs:
        copy.wait()


def fused_body(
    n, ng, velocity, stress, pier_velocity, buoyancy, layer, lame_table, shear_table, relax_table,
    impedance, footprint, damp_inverse,
):
    depth, side, line = buoyancy.shape
    own = pier_velocity.shape[1]
    piers = footprint.shape[0]
    g = lax.axis_index("gy")
    tables = jnp.stack([lame_table, shear_table, relax_table])
    onehot = layer[:, None] == jnp.arange(lame_table.shape[0], dtype=jnp.int32)[None, :]
    values = jnp.sum(jnp.where(onehot[None], tables[:, None, :], 0.0), axis=2)
    coef = jnp.broadcast_to(values[:, :, None, None], (3, depth, ROWS, LANES))
    lane = jnp.arange(LANES, dtype=jnp.int32)
    w_all = lax.dynamic_update_slice(
        jnp.zeros((depth, LANES), jnp.float32), pier_velocity, (0, g * own)
    )
    imp = lax.dynamic_update_slice(
        jnp.zeros((ROWS, LANES), jnp.float32),
        jnp.broadcast_to(impedance[None, :], (ROWS, own)), (0, g * own)
    )
    corner = jnp.pad(footprint[:, 0], (0, LANES - piers), constant_values=-line * 64)
    rows = jnp.broadcast_to((corner // line)[None, :], (ROWS, LANES))
    cols = jnp.where(lane < piers, corner % line, -64)
    cols = jnp.broadcast_to(cols[:, None], (LANES, LANES))
    f32 = jnp.float32
    hbm = pl.BlockSpec(memory_space=pl.ANY)
    vmem = pl.BlockSpec(memory_space=pltpu.VMEM)
    dma = pltpu.SemaphoreType.DMA
    tall = side + 2 * ROWS
    stage = 2 * depth + ROWS
    v, s, w = pl.pallas_call(
        functools.partial(fused, n, ng),
        out_shape=(
            jax.ShapeDtypeStruct(velocity.shape, f32),
            jax.ShapeDtypeStruct(stress.shape, f32),
            jax.ShapeDtypeStruct((depth, LANES), f32),
        ),
        in_specs=[hbm] * 4 + [vmem] * 5,
        out_specs=(hbm, hbm, vmem),
        scratch_shapes=[
            pltpu.VMEM((3, depth + 2, tall, line), f32),
            pltpu.VMEM((6, depth + 2, tall, line), f32),
            pltpu.VMEM((depth, side, line), f32),
            pltpu.VMEM((3, depth + 2, ROWS, LANES), f32),
            pltpu.VMEM((3, depth, side, line), f32),
            pltpu.VMEM((3, n * depth, ROWS, LANES), f32),
            pltpu.VMEM((3, n * depth + 2, ROWS, LANES), f32),
            pltpu.VMEM((STEPS, ng, stage, LANES), f32),
            pltpu.VMEM((depth, LANES), f32),
            pltpu.VMEM((3, depth, line), f32),
            pltpu.VMEM((3, depth, line), f32),
            pltpu.VMEM((STEPS, 3, 2, depth + 2, line), f32),
            pltpu.VMEM((STEPS, 3, 2, depth + 2, line), f32),
            dma((11,)), dma((3,)), dma((3,)), dma((2,)), dma((2,)), dma((3,)), dma((3,)),
            dma((STEPS, 3, n)), dma((STEPS, 3, n)), dma((STEPS, 3, n)), dma((STEPS, 3, n)),
            dma((STEPS, ng)), dma((STEPS, ng)), dma((STEPS, 3, 2)), dma((STEPS, 3, 2)),
            dma((9,)),
        ],
        compiler_params=pltpu.CompilerParams(
            collective_id=0, has_side_effects=True, vmem_limit_bytes=48 * 1024 * 1024
        ),
    )(velocity, stress, buoyancy, coef, w_all, imp, rows, cols, damp_inverse)
    return v, s, lax.dynamic_slice(w, (0, g * own), (depth, own))


def whole_tiles(mesh, velocity, pier_velocity):
    n, ng = mesh.shape["gx"], mesh.shape["gy"]
    depth, side, line = velocity.shape[1] // n, velocity.shape[2] // ng, velocity.shape[3]
    return (
        line % LANES == 0
        and side % ROWS == 0
        and depth % ROWS == 0
        and (side // ROWS) * (line // LANES) == n
        and pier_velocity.shape[1] <= LANES
    )


def solution(mesh):
    placed = (
        P(None, "gx", "gy", None),
        P(None, "gx", "gy", None),
        P("gx", "gy"),
        P("gx", "gy", None),
        P("gx"),
        P(),
        P(),
        P(),
        P("gy"),
        P(),
        P(),
    )

    def run(*args):
        n, ng = mesh.shape["gx"], mesh.shape["gy"]
        if whole_tiles(mesh, args[0], args[2]):
            part = functools.partial(fused_body, n, ng)
        else:
            part = body
        return mapped(part)(*args)

    def mapped(part):
        return jax.shard_map(
            part,
            mesh=mesh,
            in_specs=placed,
            out_specs=(P(None, "gx", "gy", None), P(None, "gx", "gy", None), P("gx", "gy")),
            check_vma=False,
        )

    return run
```

```python
import functools
import jax
import jax.numpy as jnp
from jax import lax
from jax.experimental import pallas as pl
from jax.experimental.pallas import tpu as pltpu
from jax.sharding import PartitionSpec as P

STEPS = 2
FOOT = 16


grid_ratio = 0.25
soil_gain = 0.2
pier_gain = 0.5


def extended(cells, sides, width):
    for axis, dim in sides:
        count = lax.axis_size(axis)
        ends = count - 1
        head = lax.slice_in_dim(cells, 0, width, axis=dim)
        tail = lax.slice_in_dim(cells, cells.shape[dim] - width, cells.shape[dim], axis=dim)
        cells = jnp.concatenate(
            [
                lax.ppermute(tail, axis, [(i, (i + 1) % count) for i in range(ends)]),
                cells,
                lax.ppermute(head, axis, [((i + 1) % count, i) for i in range(ends)]),
            ],
            axis=dim,
        )
    return cells


def forward_diff(padded, along):
    center = padded[1:-1, 1:-1, 1:-1]
    if along == 0:
        return padded[2:, 1:-1, 1:-1] - center
    if along == 1:
        return padded[1:-1, 2:, 1:-1] - center
    return padded[1:-1, 1:-1, 2:] - center


def backward_diff(padded, along):
    center = padded[1:-1, 1:-1, 1:-1]
    if along == 0:
        return center - padded[:-2, 1:-1, 1:-1]
    if along == 1:
        return center - padded[1:-1, :-2, 1:-1]
    return center - padded[1:-1, 1:-1, :-2]


def move_velocity(velocity, padded, buoyancy):
    scaled = grid_ratio * buoyancy
    first = velocity[0] + scaled * (
        backward_diff(padded[0], 2) + forward_diff(padded[3], 1) + forward_diff(padded[4], 0)
    )
    second = velocity[1] + scaled * (
        forward_diff(padded[3], 2) + backward_diff(padded[1], 1) + forward_diff(padded[5], 0)
    )
    third = velocity[2] + scaled * (
        forward_diff(padded[4], 2) + forward_diff(padded[5], 1) + backward_diff(padded[2], 0)
    )
    return jnp.stack([first, second, third])


def move_stress(stress, padded, lame_first, shear_mod, relax):
    strain_x = forward_diff(padded[0], 2)
    strain_y = forward_diff(padded[1], 1)
    strain_z = forward_diff(padded[2], 0)
    modulus = lame_first + 2.0 * shear_mod
    normal_x = relax * stress[0] + grid_ratio * (
        modulus * strain_x + lame_first * (strain_y + strain_z)
    )
    normal_y = relax * stress[1] + grid_ratio * (
        modulus * strain_y + lame_first * (strain_x + strain_z)
    )
    normal_z = relax * stress[2] + grid_ratio * (
        modulus * strain_z + lame_first * (strain_x + strain_y)
    )
    shear_xy = relax * stress[3] + grid_ratio * shear_mod * (
        backward_diff(padded[0], 1) + backward_diff(padded[1], 2)
    )
    shear_xz = relax * stress[4] + grid_ratio * shear_mod * (
        backward_diff(padded[0], 0) + backward_diff(padded[2], 2)
    )
    shear_yz = relax * stress[5] + grid_ratio * shear_mod * (
        backward_diff(padded[1], 0) + backward_diff(padded[2], 1)
    )
    return jnp.stack([normal_x, normal_y, normal_z, shear_xy, shear_xz, shear_yz])


def layer_values(layer, table):
    levels = jnp.arange(table.shape[0], dtype=jnp.int32)
    onehot = (layer[:, None] == levels[None, :]).astype(table.dtype)
    return jnp.sum(onehot * table[None, :], axis=1)[:, None, None]


def with_faces(fields):
    padded = extended(fields, (("gx", 1), ("gy", 2)), 1)
    return jnp.pad(padded, ((0, 0), (0, 0), (0, 0), (1, 1)))


def footprint_matches(cell_ids, footprint):
    piers = footprint.shape[0]
    equal = (cell_ids[:, None] == footprint.reshape(-1)[None, :]).astype(jnp.float32)
    return jnp.sum(equal.reshape(cell_ids.shape[0], piers, FOOT), axis=2)


def damp_columns(velocity, inverse):
    pencils = lax.all_to_all(velocity, "gx", split_axis=3, concat_axis=1, tiled=True)
    shape = pencils.shape
    flat = pencils.reshape(shape[0], shape[1], shape[2] * shape[3])
    damped = jnp.einsum("zk,fkm->fzm", inverse, flat, precision=lax.Precision.HIGHEST).reshape(
        shape
    )
    return lax.all_to_all(damped, "gx", split_axis=1, concat_axis=3, tiled=True)


def body(
    velocity,
    stress,
    pier_velocity,
    buoyancy,
    layer,
    lame_table,
    shear_table,
    relax_table,
    impedance,
    footprint,
    damp_inverse,
):
    depth_cells, side_cells, line_cells = (velocity.shape[1], velocity.shape[2], velocity.shape[3])
    own_piers = pier_velocity.shape[1]
    lame_first = layer_values(layer, lame_table)
    shear_mod = layer_values(layer, shear_table)
    relax = layer_values(layer, relax_table)
    row_start = lax.axis_index("gy") * side_cells
    cell_ids = row_start * line_cells + jnp.arange(side_cells * line_cells, dtype=jnp.int32)
    selector = footprint_matches(cell_ids, footprint)
    own_foot = lax.dynamic_slice_in_dim(footprint, lax.axis_index("gy") * own_piers, own_piers, 0)
    for time_step in range(STEPS):
        padded = with_faces(stress)
        velocity = move_velocity(velocity, padded, buoyancy)
        vertical = velocity[2].reshape(depth_cells, side_cells * line_cells)
        piece = lax.all_gather(velocity[2], "gy", axis=1, tiled=True)
        count = piece.shape[1]
        piece_ids = jnp.arange(count * line_cells, dtype=jnp.int32)
        picks = footprint_matches(piece_ids, own_foot)
        flat = piece.reshape(depth_cells, count * line_cells)
        summed = jnp.dot(
            flat, picks, precision=lax.Precision.HIGHEST, preferred_element_type=jnp.float32
        )
        mean_speed = summed / FOOT
        force = impedance[None, :] * (pier_velocity - mean_speed)
        pier_velocity = pier_velocity - pier_gain * force
        all_force = lax.all_gather(force, "gy", axis=1, tiled=True)
        pushed = jnp.dot(
            all_force,
            selector.T,
            precision=lax.Precision.HIGHEST,
            preferred_element_type=jnp.float32,
        )
        vertical = vertical + soil_gain * pushed
        velocity = jnp.stack(
            [velocity[0], velocity[1], vertical.reshape(depth_cells, side_cells, line_cells)]
        )
        velocity = damp_columns(velocity, damp_inverse)
        padded = with_faces(velocity)
        stress = move_stress(stress, padded, lame_first, shear_mod, relax)
    return (velocity, stress, pier_velocity)


SIDE = 4
LANES = 128
ROWS = 8
MESH = pl.DeviceIdType.MESH
Z_GHOSTS = ((2, -1), (4, 1), (5, 1))
Y_GHOSTS = ((1, -1), (3, 1), (5, 1))


def shift_x(a, ahead):
    lane = lax.broadcasted_iota(jnp.int32, a.shape, 1)
    width = a.shape[1]
    if ahead:
        return jnp.where(lane == width - 1, 0.0, pltpu.roll(a, width - 1, 1))
    return jnp.where(lane == 0, 0.0, pltpu.roll(a, 1, 1))


def fused(
    n, ng, v_hbm, s_hbm, b_hbm, coef_hbm, w_ref, imp_ref, row_ref, col_ref, damp_ref,
    v_out, s_out, w_out,
    v_ext, s_ext, buoy, coef, acc, pin, pout, um, wbuf, sg_send, sg_recv, yg_send, yg_recv,
    load_sem, zs_send, zs_recv, cf_send, cf_recv, ys_send, ys_recv,
    f_send, f_recv, r_send, r_recv, u_send, u_recv, y_send, y_recv, o_sem,
):
    me = lax.axis_index("gx")
    g = lax.axis_index("gy")
    depth, side, line = buoy.shape
    tiles = line // LANES
    inner = pl.ds(ROWS, side)

    def piece(j):
        return (
            pl.ds(pl.multiple_of((j // tiles) * ROWS, ROWS), ROWS),
            pl.ds(pl.multiple_of((j % tiles) * LANES, LANES), LANES),
        )

    loads = {}
    for slot, f in enumerate((1, 3, 5, 2, 4, 0)):
        loads[("s", f)] = pltpu.make_async_copy(
            s_hbm.at[f], s_ext.at[f, pl.ds(1, depth), inner, :], load_sem.at[slot]
        )
    loads["b"] = pltpu.make_async_copy(b_hbm, buoy, load_sem.at[6])
    for f in range(3):
        loads[("v", f)] = pltpu.make_async_copy(
            v_hbm.at[f], v_ext.at[f, pl.ds(1, depth), inner, :], load_sem.at[7 + f]
        )
    loads["c"] = pltpu.make_async_copy(coef_hbm, coef.at[:, pl.ds(1, depth)], load_sem.at[10])
    for copy in loads.values():
        copy.start()

    plane = jnp.zeros((side, line), jnp.float32)
    for f, way in Z_GHOSTS:
        s_ext[f, 0 if way < 0 else depth + 1, inner, :] = plane
    edge = jnp.zeros((ROWS, line), jnp.float32)

    def clear(k, carry):
        for f, way in Y_GHOSTS:
            s_ext[f, k, pl.ds(0 if way < 0 else ROWS + side, ROWS), :] = edge
        for f in range(3):
            v_ext[f, k, pl.ds(0, ROWS), :] = edge
            v_ext[f, k, pl.ds(ROWS + side, ROWS), :] = edge
        return carry

    lax.fori_loop(0, depth + 2, clear, 0)
    for c in range(3):
        coef[c, 0] = jnp.zeros((ROWS, LANES), jnp.float32)
        coef[c, depth + 1] = jnp.zeros((ROWS, LANES), jnp.float32)
        pout[c, 0] = jnp.zeros((ROWS, LANES), jnp.float32)
        pout[c, n * depth + 1] = jnp.zeros((ROWS, LANES), jnp.float32)

    barrier = pltpu.get_barrier_semaphore()
    for d in range(1, n):
        pl.semaphore_signal(
            barrier, inc=1, device_id=(lax.rem(me + d, n), g), device_id_type=MESH
        )
    for d in range(1, ng):
        pl.semaphore_signal(
            barrier, inc=1, device_id=(me, lax.rem(g + d, ng)), device_id_type=MESH
        )
    pl.semaphore_wait(barrier, n - 1 + ng - 1)

    def z_copy(i):
        f, way = Z_GHOSTS[i]
        return pltpu.make_async_remote_copy(
            src_ref=s_hbm.at[f, depth - 1 if way < 0 else 0],
            dst_ref=s_ext.at[f, 0 if way < 0 else depth + 1, inner, :],
            send_sem=zs_send.at[i],
            recv_sem=zs_recv.at[i],
            device_id=(me - way, g),
            device_id_type=MESH,
        )

    def c_copy(way):
        i = (way + 1) // 2
        return pltpu.make_async_remote_copy(
            src_ref=coef_hbm.at[:, depth - 1 if way < 0 else 0],
            dst_ref=coef.at[:, 0 if way < 0 else depth + 1],
            send_sem=cf_send.at[i],
            recv_sem=cf_recv.at[i],
            device_id=(me - way, g),
            device_id_type=MESH,
        )

    def y_stress(i):
        f, way = Y_GHOSTS[i]
        return pltpu.make_async_remote_copy(
            src_ref=sg_send.at[i],
            dst_ref=sg_recv.at[i],
            send_sem=ys_send.at[i],
            recv_sem=ys_recv.at[i],
            device_id=(me, g - way),
            device_id_type=MESH,
        )

    not_ends = {
        -1: (me > 0, me < n - 1, g > 0, g < ng - 1),
        1: (me < n - 1, me > 0, g < ng - 1, g > 0),
    }

    for i, (f, way) in enumerate(Z_GHOSTS):
        @pl.when(not_ends[way][1])
        def _(i=i):
            z_copy(i).start()
    for way in (-1, 1):
        @pl.when(not_ends[way][1])
        def _(way=way):
            c_copy(way).start()
    for i, (f, way) in enumerate(Y_GHOSTS):
        loads[("s", f)].wait()
        sg_send[i] = s_ext[f, pl.ds(1, depth), ROWS + side - 1 if way < 0 else ROWS, :]

        @pl.when(not_ends[way][3])
        def _(i=i):
            y_stress(i).start()
    for key, copy in loads.items():
        if key not in (("s", 1), ("s", 3), ("s", 5)):
            copy.wait()

    ids = lax.broadcasted_iota(jnp.int32, (side, LANES), 0) + g * side
    first = row_ref[0:1, :]
    in_rows = jnp.where((ids >= first) & (ids < first + SIDE), 1.0, 0.0)
    across = lax.broadcasted_iota(jnp.int32, (LANES, line), 1)
    start = jnp.concatenate([col_ref[...]] * tiles, axis=1)
    in_cols = jnp.where((across >= start) & (across < start + SIDE), 1.0, 0.0)

    for i, (f, way) in enumerate(Z_GHOSTS):
        @pl.when(not_ends[way][0])
        def _(i=i):
            z_copy(i).wait_recv()

        @pl.when(not_ends[way][1])
        def _(i=i):
            z_copy(i).wait_send()
    for way in (-1, 1):
        @pl.when(not_ends[way][0])
        def _(way=way):
            c_copy(way).wait_recv()

        @pl.when(not_ends[way][1])
        def _(way=way):
            c_copy(way).wait_send()
    for i, (f, way) in enumerate(Y_GHOSTS):
        @pl.when(not_ends[way][2])
        def _(i=i, f=f, way=way):
            y_stress(i).wait_recv()
            s_ext[f, pl.ds(1, depth), ROWS - 1 if way < 0 else ROWS + side, :] = sg_recv[i]

        @pl.when(not_ends[way][3])
        def _(i=i):
            y_stress(i).wait_send()

    def cells(ref, f, k, shift=0, begin=ROWS, rows=None):
        return ref[f, k, pl.ds(begin + shift, side if rows is None else rows), :]

    def speed_x(i, carry):
        k = i + 1
        xx, xy, xz = cells(s_ext, 0, k), cells(s_ext, 3, k), cells(s_ext, 4, k)
        total = (xx - shift_x(xx, False)) + (cells(s_ext, 3, k, 1) - xy)
        total = total + (cells(s_ext, 4, k + 1) - xz)
        acc[0, i] = cells(v_ext, 0, k) + (grid_ratio * buoy[i]) * total
        return carry

    def speed_y(i, carry):
        k = i + 1
        xy, yy, yz = cells(s_ext, 3, k), cells(s_ext, 1, k), cells(s_ext, 5, k)
        total = (shift_x(xy, True) - xy) + (yy - cells(s_ext, 1, k, -1))
        total = total + (cells(s_ext, 5, k + 1) - yz)
        acc[1, i] = cells(v_ext, 1, k) + (grid_ratio * buoy[i]) * total
        return carry

    def speed_z(i, carry):
        k = i + 1
        xz, yz, zz = cells(s_ext, 4, k), cells(s_ext, 5, k), cells(s_ext, 2, k)
        total = (shift_x(xz, True) - xz) + (cells(s_ext, 5, k, 1) - yz)
        total = total + (zz - cells(s_ext, 2, k - 1))
        acc[2, i] = cells(v_ext, 2, k) + (grid_ratio * buoy[i]) * total
        return carry

    def wide(c, k, rows):
        tile = jnp.concatenate([coef[c, k]] * tiles, axis=1)
        return jnp.concatenate([tile] * (rows // ROWS), axis=0)

    def normals(k, begin, rows):
        at = functools.partial(cells, begin=begin, rows=rows)
        lame, shear, relax = (wide(c, k, rows) for c in range(3))
        vx, vy, vz = at(v_ext, 0, k), at(v_ext, 1, k), at(v_ext, 2, k)
        ex = shift_x(vx, True) - vx
        ey = at(v_ext, 1, k, 1) - vy
        ez = at(v_ext, 2, k + 1) - vz
        modulus = lame + 2.0 * shear
        for f, own, others in ((0, ex, ey + ez), (1, ey, ex + ez), (2, ez, ex + ey)):
            s_ext[f, k, pl.ds(begin, rows), :] = relax * at(s_ext, f, k) + grid_ratio * (
                modulus * own + lame * others
            )

    def shears(k, begin, rows, which):
        at = functools.partial(cells, begin=begin, rows=rows)
        shear, relax = grid_ratio * wide(1, k, rows), wide(2, k, rows)
        for f in which:
            if f == 3:
                vy = at(v_ext, 1, k)
                strain = (at(v_ext, 0, k) - at(v_ext, 0, k, -1)) + (vy - shift_x(vy, False))
            elif f == 4:
                vz = at(v_ext, 2, k)
                strain = (at(v_ext, 0, k) - at(v_ext, 0, k - 1)) + (vz - shift_x(vz, False))
            else:
                strain = (at(v_ext, 1, k) - at(v_ext, 1, k - 1)) + (
                    at(v_ext, 2, k) - at(v_ext, 2, k, -1)
                )
            s_ext[f, k, pl.ds(begin, rows), :] = relax * at(s_ext, f, k) + shear * strain

    def there(step, f, d):
        t = lax.rem(me + d, n)
        ys, xs = piece(t)
        src = acc.at[f, :, ys, xs]
        dst = pin.at[f, pl.ds(me * depth, depth)]
        if d == 0:
            return pltpu.make_async_copy(src, dst, f_recv.at[step, f, 0])
        return pltpu.make_async_remote_copy(
            src_ref=src, dst_ref=dst, send_sem=f_send.at[step, f, d],
            recv_sem=f_recv.at[step, f, d], device_id=(t, g), device_id_type=MESH,
        )

    def back(step, f, d):
        t = lax.rem(me + d, n)
        ys, xs = pl.ds(pl.multiple_of((me // tiles) * ROWS + ROWS, ROWS), ROWS), piece(me)[1]
        src = pout.at[f, pl.ds(t * depth, depth + 2)]
        dst = v_ext.at[f, :, ys, xs]
        if d == 0:
            return pltpu.make_async_copy(src, dst, r_recv.at[step, f, 0])
        return pltpu.make_async_remote_copy(
            src_ref=src, dst_ref=dst, send_sem=r_send.at[step, f, d],
            recv_sem=r_recv.at[step, f, d], device_id=(t, g), device_id_type=MESH,
        )

    def start_all(make, step, f):
        for d in list(range(1, n)) + [0]:
            make(step, f, d).start()

    def wait_sent(make, step, f):
        for d in range(1, n):
            make(step, f, d).wait_send()

    def wait_got(make, step, f):
        make(step, f, 0).wait()
        for d in range(1, n):
            make(step, f, d).wait_recv()

    def share(step, d):
        return pltpu.make_async_remote_copy(
            src_ref=um.at[step, 0], dst_ref=um.at[step, d],
            send_sem=u_send.at[step, d], recv_sem=u_recv.at[step, d],
            device_id=(me, lax.rem(g + d, ng)), device_id_type=MESH,
        )

    def y_speed(step, f, i):
        return pltpu.make_async_remote_copy(
            src_ref=yg_send.at[step, f, i], dst_ref=yg_recv.at[step, f, i],
            send_sem=y_send.at[step, f, i], recv_sem=y_recv.at[step, f, i],
            device_id=(me, g + 1 - 2 * i), device_id_type=MESH,
        )

    has_next, has_last = g < ng - 1, g > 0
    planes = pl.ds(0, depth + 2)

    def stress_xy():
        def at(i, carry):
            shears(i + 1, ROWS, ROWS + side, (3,))
            return carry

        lax.fori_loop(0, depth, at, 0)

        @pl.when(g == ng - 1)
        def _():
            s_ext[3, planes, ROWS + side, :] = jnp.zeros((depth + 2, line), jnp.float32)

    def stress_xz():
        def at(i, carry):
            normals(i, 0, ROWS + side)
            shears(i + 1, ROWS, side, (4,))
            return carry

        lax.fori_loop(0, depth + 1, at, 0)

        @pl.when(g == 0)
        def _():
            s_ext[1, planes, ROWS - 1, :] = jnp.zeros((depth + 2, line), jnp.float32)

    def stress_yz():
        def at(i, carry):
            shears(i + 1, ROWS, ROWS + side, (5,))
            return carry

        lax.fori_loop(0, depth + 1, at, 0)

        @pl.when(g == ng - 1)
        def _():
            s_ext[5, planes, ROWS + side, :] = jnp.zeros((depth + 2, line), jnp.float32)

    def v_copy(f):
        return pltpu.make_async_copy(
            v_ext.at[f, pl.ds(1, depth), inner, :], v_out.at[f], o_sem.at[f]
        )

    def out_copy(f):
        return pltpu.make_async_copy(
            s_ext.at[f, pl.ds(1, depth), inner, :], s_out.at[f], o_sem.at[3 + f]
        )

    for step in range(STEPS):
        if step > 0:
            for f in range(3):
                wait_sent(there, step - 1, f)
        if step > 0:
            stress_xz()
        lax.fori_loop(0, depth, speed_x, 0)
        start_all(there, step, 0)
        if step > 0:
            stress_yz()
        lax.fori_loop(0, depth, speed_y, 0)
        start_all(there, step, 1)
        lax.fori_loop(0, depth, speed_z, 0)
        flat = acc[2].reshape(depth * side, line)
        part = lax.dot_general(
            flat, in_cols, (((1,), (1,)), ((), ())),
            precision=lax.Precision.HIGHEST, preferred_element_type=jnp.float32,
        ).reshape(depth, side, LANES)
        um[step, 0, pl.ds(0, depth), :] = jnp.sum(part * in_rows[None], axis=1)
        um[step, 0, pl.ds(depth, depth), :] = w_ref[...]
        um[step, 0, pl.ds(2 * depth, ROWS), :] = imp_ref[...]
        for d in range(1, ng):
            share(step, d).start()
        for d in range(1, ng):
            share(step, d).wait()
        every = um[step, 0]
        for d in range(1, ng):
            every = every + um[step, d]
        w = every[depth : 2 * depth] if step == 0 else wbuf[...]
        force = every[2 * depth : 2 * depth + 1] * (w - every[0:depth] / FOOT)
        wbuf[...] = w - pier_gain * force
        spread = (force[:, None, :] * in_rows[None]).reshape(depth * side, LANES)
        pushed = jnp.dot(
            spread, in_cols, precision=lax.Precision.HIGHEST, preferred_element_type=jnp.float32
        )
        acc[2] = acc[2] + soil_gain * pushed.reshape(depth, side, line)
        start_all(there, step, 2)

        for f in range(3):
            wait_got(there, step, f)
            if step > 0:
                wait_sent(back, step - 1, f)
            full = jnp.concatenate([pin[f, :, y, :] for y in range(ROWS)], axis=1)
            damped = jnp.dot(
                damp_ref[...], full, precision=lax.Precision.HIGHEST,
                preferred_element_type=jnp.float32,
            )
            for y in range(ROWS):
                pout[f, pl.ds(1, n * depth), y, :] = damped[:, y * LANES : (y + 1) * LANES]
            start_all(back, step, f)
        def arrive(f, step=step):
            wait_got(back, step, f)
            yg_send[step, f, 0] = v_ext[f, planes, ROWS + side - 1, :]
            yg_send[step, f, 1] = v_ext[f, planes, ROWS, :]

            @pl.when(has_next)
            def _():
                y_speed(step, f, 0).start()

            @pl.when(has_last)
            def _():
                y_speed(step, f, 1).start()
            if step == STEPS - 1:
                v_copy(f).start()

        def edges(f, step=step):
            @pl.when(has_last)
            def _():
                y_speed(step, f, 0).wait_recv()
                v_ext[f, planes, ROWS - 1, :] = yg_recv[step, f, 0]
                y_speed(step, f, 1).wait_send()

            @pl.when(has_next)
            def _():
                y_speed(step, f, 1).wait_recv()
                v_ext[f, planes, ROWS + side, :] = yg_recv[step, f, 1]
                y_speed(step, f, 0).wait_send()

        arrive(0)
        arrive(1)
        edges(0)
        edges(1)
        if step < STEPS - 1:
            stress_xy()
            arrive(2)
            edges(2)
        else:
            def last_xy(i, carry):
                shears(i + 1, ROWS, side, (3,))
                return carry

            def last_shears(i, carry):
                shears(i + 1, ROWS, side, (4, 5))
                return carry

            def last_normals(i, carry):
                normals(i + 1, ROWS, side)
                return carry

            lax.fori_loop(0, depth, last_xy, 0)
            out_copy(3).start()
            arrive(2)
            edges(2)
            lax.fori_loop(0, depth, last_shears, 0)
            out_copy(4).start()
            out_copy(5).start()
            lax.fori_loop(0, depth, last_normals, 0)
            for f in range(3):
                out_copy(f).start()

    w_out[...] = wbuf[...]
    for f in range(3):
        wait_sent(there, STEPS - 1, f)
        wait_sent(back, STEPS - 1, f)
    for f in range(3):
        v_copy(f).wait()
    for f in range(6):
        out_copy(f).wait()


def fused_body(
    n, ng, velocity, stress, pier_velocity, buoyancy, layer, lame_table, shear_table, relax_table,
    impedance, footprint, damp_inverse,
):
    depth, side, line = buoyancy.shape
    own = pier_velocity.shape[1]
    piers = footprint.shape[0]
    g = lax.axis_index("gy")
    tables = jnp.stack([lame_table, shear_table, relax_table])
    onehot = layer[:, None] == jnp.arange(lame_table.shape[0], dtype=jnp.int32)[None, :]
    values = jnp.sum(jnp.where(onehot[None], tables[:, None, :], 0.0), axis=2)
    coef = jnp.broadcast_to(values[:, :, None, None], (3, depth, ROWS, LANES))
    lane = jnp.arange(LANES, dtype=jnp.int32)
    w_all = lax.dynamic_update_slice(
        jnp.zeros((depth, LANES), jnp.float32), pier_velocity, (0, g * own)
    )
    imp = lax.dynamic_update_slice(
        jnp.zeros((ROWS, LANES), jnp.float32),
        jnp.broadcast_to(impedance[None, :], (ROWS, own)), (0, g * own)
    )
    corner = jnp.pad(footprint[:, 0], (0, LANES - piers), constant_values=-line * 64)
    rows = jnp.broadcast_to((corner // line)[None, :], (ROWS, LANES))
    cols = jnp.where(lane < piers, corner % line, -64)
    cols = jnp.broadcast_to(cols[:, None], (LANES, LANES))
    f32 = jnp.float32
    hbm = pl.BlockSpec(memory_space=pl.ANY)
    vmem = pl.BlockSpec(memory_space=pltpu.VMEM)
    dma = pltpu.SemaphoreType.DMA
    tall = side + 2 * ROWS
    stage = 2 * depth + ROWS
    v, s, w = pl.pallas_call(
        functools.partial(fused, n, ng),
        out_shape=(
            jax.ShapeDtypeStruct(velocity.shape, f32),
            jax.ShapeDtypeStruct(stress.shape, f32),
            jax.ShapeDtypeStruct((depth, LANES), f32),
        ),
        in_specs=[hbm] * 4 + [vmem] * 5,
        out_specs=(hbm, hbm, vmem),
        scratch_shapes=[
            pltpu.VMEM((3, depth + 2, tall, line), f32),
            pltpu.VMEM((6, depth + 2, tall, line), f32),
            pltpu.VMEM((depth, side, line), f32),
            pltpu.VMEM((3, depth + 2, ROWS, LANES), f32),
            pltpu.VMEM((3, depth, side, line), f32),
            pltpu.VMEM((3, n * depth, ROWS, LANES), f32),
            pltpu.VMEM((3, n * depth + 2, ROWS, LANES), f32),
            pltpu.VMEM((STEPS, ng, stage, LANES), f32),
            pltpu.VMEM((depth, LANES), f32),
            pltpu.VMEM((3, depth, line), f32),
            pltpu.VMEM((3, depth, line), f32),
            pltpu.VMEM((STEPS, 3, 2, depth + 2, line), f32),
            pltpu.VMEM((STEPS, 3, 2, depth + 2, line), f32),
            dma((11,)), dma((3,)), dma((3,)), dma((2,)), dma((2,)), dma((3,)), dma((3,)),
            dma((STEPS, 3, n)), dma((STEPS, 3, n)), dma((STEPS, 3, n)), dma((STEPS, 3, n)),
            dma((STEPS, ng)), dma((STEPS, ng)), dma((STEPS, 3, 2)), dma((STEPS, 3, 2)),
            dma((9,)),
        ],
        compiler_params=pltpu.CompilerParams(
            collective_id=0, has_side_effects=True, vmem_limit_bytes=60 * 1024 * 1024
        ),
    )(velocity, stress, buoyancy, coef, w_all, imp, rows, cols, damp_inverse)
    return v, s, lax.dynamic_slice(w, (0, g * own), (depth, own))


def whole_tiles(mesh, velocity, pier_velocity):
    n, ng = mesh.shape["gx"], mesh.shape["gy"]
    depth, side, line = velocity.shape[1] // n, velocity.shape[2] // ng, velocity.shape[3]
    return (
        line % LANES == 0
        and side % ROWS == 0
        and depth % ROWS == 0
        and (side // ROWS) * (line // LANES) == n
        and pier_velocity.shape[1] <= LANES
    )


def solution(mesh):
    placed = (
        P(None, "gx", "gy", None),
        P(None, "gx", "gy", None),
        P("gx", "gy"),
        P("gx", "gy", None),
        P("gx"),
        P(),
        P(),
        P(),
        P("gy"),
        P(),
        P(),
    )

    def run(*args):
        n, ng = mesh.shape["gx"], mesh.shape["gy"]
        if whole_tiles(mesh, args[0], args[2]):
            part = functools.partial(fused_body, n, ng)
        else:
            part = body
        return mapped(part)(*args)

    def mapped(part):
        return jax.shard_map(
            part,
            mesh=mesh,
            in_specs=placed,
            out_specs=(P(None, "gx", "gy", None), P(None, "gx", "gy", None), P("gx", "gy")),
            check_vma=False,
        )

    return run
```

```python
import functools
import jax
import jax.numpy as jnp
from jax import lax
from jax.experimental import pallas as pl
from jax.experimental.pallas import tpu as pltpu
from jax.sharding import PartitionSpec as P

STEPS = 2
FOOT = 16


grid_ratio = 0.25
soil_gain = 0.2
pier_gain = 0.5


def extended(cells, sides, width):
    for axis, dim in sides:
        count = lax.axis_size(axis)
        ends = count - 1
        head = lax.slice_in_dim(cells, 0, width, axis=dim)
        tail = lax.slice_in_dim(cells, cells.shape[dim] - width, cells.shape[dim], axis=dim)
        cells = jnp.concatenate(
            [
                lax.ppermute(tail, axis, [(i, (i + 1) % count) for i in range(ends)]),
                cells,
                lax.ppermute(head, axis, [((i + 1) % count, i) for i in range(ends)]),
            ],
            axis=dim,
        )
    return cells


def forward_diff(padded, along):
    center = padded[1:-1, 1:-1, 1:-1]
    if along == 0:
        return padded[2:, 1:-1, 1:-1] - center
    if along == 1:
        return padded[1:-1, 2:, 1:-1] - center
    return padded[1:-1, 1:-1, 2:] - center


def backward_diff(padded, along):
    center = padded[1:-1, 1:-1, 1:-1]
    if along == 0:
        return center - padded[:-2, 1:-1, 1:-1]
    if along == 1:
        return center - padded[1:-1, :-2, 1:-1]
    return center - padded[1:-1, 1:-1, :-2]


def move_velocity(velocity, padded, buoyancy):
    scaled = grid_ratio * buoyancy
    first = velocity[0] + scaled * (
        backward_diff(padded[0], 2) + forward_diff(padded[3], 1) + forward_diff(padded[4], 0)
    )
    second = velocity[1] + scaled * (
        forward_diff(padded[3], 2) + backward_diff(padded[1], 1) + forward_diff(padded[5], 0)
    )
    third = velocity[2] + scaled * (
        forward_diff(padded[4], 2) + forward_diff(padded[5], 1) + backward_diff(padded[2], 0)
    )
    return jnp.stack([first, second, third])


def move_stress(stress, padded, lame_first, shear_mod, relax):
    strain_x = forward_diff(padded[0], 2)
    strain_y = forward_diff(padded[1], 1)
    strain_z = forward_diff(padded[2], 0)
    modulus = lame_first + 2.0 * shear_mod
    normal_x = relax * stress[0] + grid_ratio * (
        modulus * strain_x + lame_first * (strain_y + strain_z)
    )
    normal_y = relax * stress[1] + grid_ratio * (
        modulus * strain_y + lame_first * (strain_x + strain_z)
    )
    normal_z = relax * stress[2] + grid_ratio * (
        modulus * strain_z + lame_first * (strain_x + strain_y)
    )
    shear_xy = relax * stress[3] + grid_ratio * shear_mod * (
        backward_diff(padded[0], 1) + backward_diff(padded[1], 2)
    )
    shear_xz = relax * stress[4] + grid_ratio * shear_mod * (
        backward_diff(padded[0], 0) + backward_diff(padded[2], 2)
    )
    shear_yz = relax * stress[5] + grid_ratio * shear_mod * (
        backward_diff(padded[1], 0) + backward_diff(padded[2], 1)
    )
    return jnp.stack([normal_x, normal_y, normal_z, shear_xy, shear_xz, shear_yz])


def layer_values(layer, table):
    levels = jnp.arange(table.shape[0], dtype=jnp.int32)
    onehot = (layer[:, None] == levels[None, :]).astype(table.dtype)
    return jnp.sum(onehot * table[None, :], axis=1)[:, None, None]


def with_faces(fields):
    padded = extended(fields, (("gx", 1), ("gy", 2)), 1)
    return jnp.pad(padded, ((0, 0), (0, 0), (0, 0), (1, 1)))


def footprint_matches(cell_ids, footprint):
    piers = footprint.shape[0]
    equal = (cell_ids[:, None] == footprint.reshape(-1)[None, :]).astype(jnp.float32)
    return jnp.sum(equal.reshape(cell_ids.shape[0], piers, FOOT), axis=2)


def damp_columns(velocity, inverse):
    pencils = lax.all_to_all(velocity, "gx", split_axis=3, concat_axis=1, tiled=True)
    shape = pencils.shape
    flat = pencils.reshape(shape[0], shape[1], shape[2] * shape[3])
    damped = jnp.einsum("zk,fkm->fzm", inverse, flat, precision=lax.Precision.HIGHEST).reshape(
        shape
    )
    return lax.all_to_all(damped, "gx", split_axis=1, concat_axis=3, tiled=True)


def body(
    velocity,
    stress,
    pier_velocity,
    buoyancy,
    layer,
    lame_table,
    shear_table,
    relax_table,
    impedance,
    footprint,
    damp_inverse,
):
    depth_cells, side_cells, line_cells = (velocity.shape[1], velocity.shape[2], velocity.shape[3])
    own_piers = pier_velocity.shape[1]
    lame_first = layer_values(layer, lame_table)
    shear_mod = layer_values(layer, shear_table)
    relax = layer_values(layer, relax_table)
    row_start = lax.axis_index("gy") * side_cells
    cell_ids = row_start * line_cells + jnp.arange(side_cells * line_cells, dtype=jnp.int32)
    selector = footprint_matches(cell_ids, footprint)
    own_foot = lax.dynamic_slice_in_dim(footprint, lax.axis_index("gy") * own_piers, own_piers, 0)
    for time_step in range(STEPS):
        padded = with_faces(stress)
        velocity = move_velocity(velocity, padded, buoyancy)
        vertical = velocity[2].reshape(depth_cells, side_cells * line_cells)
        piece = lax.all_gather(velocity[2], "gy", axis=1, tiled=True)
        count = piece.shape[1]
        piece_ids = jnp.arange(count * line_cells, dtype=jnp.int32)
        picks = footprint_matches(piece_ids, own_foot)
        flat = piece.reshape(depth_cells, count * line_cells)
        summed = jnp.dot(
            flat, picks, precision=lax.Precision.HIGHEST, preferred_element_type=jnp.float32
        )
        mean_speed = summed / FOOT
        force = impedance[None, :] * (pier_velocity - mean_speed)
        pier_velocity = pier_velocity - pier_gain * force
        all_force = lax.all_gather(force, "gy", axis=1, tiled=True)
        pushed = jnp.dot(
            all_force,
            selector.T,
            precision=lax.Precision.HIGHEST,
            preferred_element_type=jnp.float32,
        )
        vertical = vertical + soil_gain * pushed
        velocity = jnp.stack(
            [velocity[0], velocity[1], vertical.reshape(depth_cells, side_cells, line_cells)]
        )
        velocity = damp_columns(velocity, damp_inverse)
        padded = with_faces(velocity)
        stress = move_stress(stress, padded, lame_first, shear_mod, relax)
    return (velocity, stress, pier_velocity)


SIDE = 4
LANES = 128
ROWS = 8
MESH = pl.DeviceIdType.MESH
Z_GHOSTS = ((2, -1), (4, 1), (5, 1))
Y_GHOSTS = ((1, -1), (3, 1), (5, 1))


def shift_x(a, ahead):
    lane = lax.broadcasted_iota(jnp.int32, a.shape, 1)
    width = a.shape[1]
    if ahead:
        return jnp.where(lane == width - 1, 0.0, pltpu.roll(a, width - 1, 1))
    return jnp.where(lane == 0, 0.0, pltpu.roll(a, 1, 1))


def fused(
    n, ng, v_hbm, s_hbm, b_hbm, layer_ref, lame_ref, shear_ref, relax_ref, w_ref, imp_ref, row_ref, col_ref, damp_ref,
    v_out, s_out, w_out,
    v_ext, s_ext, buoy, coef, acc, pin, pout, um, wbuf, sg_send, sg_recv, yg_send, yg_recv,
    load_sem, zs_send, zs_recv, cf_send, cf_recv, ys_send, ys_recv,
    f_send, f_recv, r_send, r_recv, u_send, u_recv, y_send, y_recv, o_sem,
):
    me = lax.axis_index("gx")
    g = lax.axis_index("gy")
    depth, side, line = buoy.shape
    tiles = line // LANES
    inner = pl.ds(ROWS, side)

    def piece(j):
        return (
            pl.ds(pl.multiple_of((j // tiles) * ROWS, ROWS), ROWS),
            pl.ds(pl.multiple_of((j % tiles) * LANES, LANES), LANES),
        )

    loads = {}
    for slot, f in enumerate((1, 3, 5, 2, 4, 0)):
        loads[("s", f)] = pltpu.make_async_copy(
            s_hbm.at[f], s_ext.at[f, pl.ds(1, depth), inner, :], load_sem.at[slot]
        )
    loads["b"] = pltpu.make_async_copy(b_hbm, buoy, load_sem.at[6])
    for f in range(3):
        loads[("v", f)] = pltpu.make_async_copy(
            v_hbm.at[f], v_ext.at[f, pl.ds(1, depth), inner, :], load_sem.at[7 + f]
        )
    for copy in loads.values():
        copy.start()

    plane = jnp.zeros((side, line), jnp.float32)
    for f, way in Z_GHOSTS:
        s_ext[f, 0 if way < 0 else depth + 1, inner, :] = plane
    edge = jnp.zeros((ROWS, line), jnp.float32)

    def clear(k, carry):
        for f, way in Y_GHOSTS:
            s_ext[f, k, pl.ds(0 if way < 0 else ROWS + side, ROWS), :] = edge
        for f in range(3 * STEPS):
            v_ext[f, k, pl.ds(0, ROWS), :] = edge
            v_ext[f, k, pl.ds(ROWS + side, ROWS), :] = edge
        return carry

    lax.fori_loop(0, depth + 2, clear, 0)
    for k in range(depth):
        for c, table in enumerate((lame_ref, shear_ref, relax_ref)):
            coef[c, k + 1] = jnp.full((ROWS, LANES), table[layer_ref[k]], jnp.float32)
    for c in range(3):
        coef[c, 0] = jnp.zeros((ROWS, LANES), jnp.float32)
        coef[c, depth + 1] = jnp.zeros((ROWS, LANES), jnp.float32)
        pout[c, 0] = jnp.zeros((ROWS, LANES), jnp.float32)
        pout[c, n * depth + 1] = jnp.zeros((ROWS, LANES), jnp.float32)

    barrier = pltpu.get_barrier_semaphore()
    for d in range(1, n):
        pl.semaphore_signal(
            barrier, inc=1, device_id=(lax.rem(me + d, n), g), device_id_type=MESH
        )
    for d in range(1, ng):
        pl.semaphore_signal(
            barrier, inc=1, device_id=(me, lax.rem(g + d, ng)), device_id_type=MESH
        )
    pl.semaphore_wait(barrier, n - 1 + ng - 1)

    def z_copy(i):
        f, way = Z_GHOSTS[i]
        return pltpu.make_async_remote_copy(
            src_ref=s_hbm.at[f, depth - 1 if way < 0 else 0],
            dst_ref=s_ext.at[f, 0 if way < 0 else depth + 1, inner, :],
            send_sem=zs_send.at[i],
            recv_sem=zs_recv.at[i],
            device_id=(me - way, g),
            device_id_type=MESH,
        )

    def c_copy(way):
        i = (way + 1) // 2
        return pltpu.make_async_remote_copy(
            src_ref=coef.at[:, depth if way < 0 else 1],
            dst_ref=coef.at[:, 0 if way < 0 else depth + 1],
            send_sem=cf_send.at[i],
            recv_sem=cf_recv.at[i],
            device_id=(me - way, g),
            device_id_type=MESH,
        )

    def y_stress(i):
        f, way = Y_GHOSTS[i]
        return pltpu.make_async_remote_copy(
            src_ref=sg_send.at[i],
            dst_ref=sg_recv.at[i],
            send_sem=ys_send.at[i],
            recv_sem=ys_recv.at[i],
            device_id=(me, g - way),
            device_id_type=MESH,
        )

    not_ends = {
        -1: (me > 0, me < n - 1, g > 0, g < ng - 1),
        1: (me < n - 1, me > 0, g < ng - 1, g > 0),
    }

    for i, (f, way) in enumerate(Z_GHOSTS):
        @pl.when(not_ends[way][1])
        def _(i=i):
            z_copy(i).start()
    for way in (-1, 1):
        @pl.when(not_ends[way][1])
        def _(way=way):
            c_copy(way).start()
    for i, (f, way) in enumerate(Y_GHOSTS):
        loads[("s", f)].wait()
        sg_send[i] = s_ext[f, pl.ds(1, depth), ROWS + side - 1 if way < 0 else ROWS, :]

        @pl.when(not_ends[way][3])
        def _(i=i):
            y_stress(i).start()
    for key, copy in loads.items():
        if key not in (("s", 1), ("s", 3), ("s", 5)):
            copy.wait()

    ids = lax.broadcasted_iota(jnp.int32, (side, LANES), 0) + g * side
    first = row_ref[0:1, :]
    in_rows = jnp.where((ids >= first) & (ids < first + SIDE), 1.0, 0.0)
    across = lax.broadcasted_iota(jnp.int32, (LANES, line), 1)
    start = jnp.concatenate([col_ref[...]] * tiles, axis=1)
    in_cols = jnp.where((across >= start) & (across < start + SIDE), 1.0, 0.0)

    for i, (f, way) in enumerate(Z_GHOSTS):
        @pl.when(not_ends[way][0])
        def _(i=i):
            z_copy(i).wait_recv()

        @pl.when(not_ends[way][1])
        def _(i=i):
            z_copy(i).wait_send()
    for way in (-1, 1):
        @pl.when(not_ends[way][0])
        def _(way=way):
            c_copy(way).wait_recv()

        @pl.when(not_ends[way][1])
        def _(way=way):
            c_copy(way).wait_send()
    for i, (f, way) in enumerate(Y_GHOSTS):
        @pl.when(not_ends[way][2])
        def _(i=i, f=f, way=way):
            y_stress(i).wait_recv()
            s_ext[f, pl.ds(1, depth), ROWS - 1 if way < 0 else ROWS + side, :] = sg_recv[i]

        @pl.when(not_ends[way][3])
        def _(i=i):
            y_stress(i).wait_send()

    def cells(ref, f, k, shift=0, begin=ROWS, rows=None):
        return ref[f, k, pl.ds(begin + shift, side if rows is None else rows), :]

    base = [0]

    def speed_x(i, carry):
        k = i + 1
        xx, xy, xz = cells(s_ext, 0, k), cells(s_ext, 3, k), cells(s_ext, 4, k)
        total = (xx - shift_x(xx, False)) + (cells(s_ext, 3, k, 1) - xy)
        total = total + (cells(s_ext, 4, k + 1) - xz)
        acc[0, i] = cells(v_ext, base[0] + 0, k) + (grid_ratio * buoy[i]) * total
        return carry

    def speed_y(i, carry):
        k = i + 1
        xy, yy, yz = cells(s_ext, 3, k), cells(s_ext, 1, k), cells(s_ext, 5, k)
        total = (shift_x(xy, True) - xy) + (yy - cells(s_ext, 1, k, -1))
        total = total + (cells(s_ext, 5, k + 1) - yz)
        acc[1, i] = cells(v_ext, base[0] + 1, k) + (grid_ratio * buoy[i]) * total
        return carry

    def speed_z(i, carry):
        k = i + 1
        xz, yz, zz = cells(s_ext, 4, k), cells(s_ext, 5, k), cells(s_ext, 2, k)
        total = (shift_x(xz, True) - xz) + (cells(s_ext, 5, k, 1) - yz)
        total = total + (zz - cells(s_ext, 2, k - 1))
        acc[2, i] = cells(v_ext, base[0] + 2, k) + (grid_ratio * buoy[i]) * total
        return carry

    def wide(c, k, rows):
        tile = jnp.concatenate([coef[c, k]] * tiles, axis=1)
        return jnp.concatenate([tile] * (rows // ROWS), axis=0)

    def normals(k, begin, rows, which=(0, 1, 2)):
        at = functools.partial(cells, begin=begin, rows=rows)
        lame, shear, relax = (wide(c, k, rows) for c in range(3))
        vx, vy, vz = at(v_ext, base[0] + 0, k), at(v_ext, base[0] + 1, k), at(v_ext, base[0] + 2, k)
        ex = shift_x(vx, True) - vx
        ey = at(v_ext, base[0] + 1, k, 1) - vy
        ez = at(v_ext, base[0] + 2, k + 1) - vz
        modulus = lame + 2.0 * shear
        for f in which:
            own, others = ((ex, ey + ez), (ey, ex + ez), (ez, ex + ey))[f]
            s_ext[f, k, pl.ds(begin, rows), :] = relax * at(s_ext, f, k) + grid_ratio * (
                modulus * own + lame * others
            )

    def shears(k, begin, rows, which):
        at = functools.partial(cells, begin=begin, rows=rows)
        shear, relax = grid_ratio * wide(1, k, rows), wide(2, k, rows)
        for f in which:
            if f == 3:
                vy = at(v_ext, base[0] + 1, k)
                strain = (at(v_ext, base[0] + 0, k) - at(v_ext, base[0] + 0, k, -1)) + (vy - shift_x(vy, False))
            elif f == 4:
                vz = at(v_ext, base[0] + 2, k)
                strain = (at(v_ext, base[0] + 0, k) - at(v_ext, base[0] + 0, k - 1)) + (vz - shift_x(vz, False))
            else:
                strain = (at(v_ext, base[0] + 1, k) - at(v_ext, base[0] + 1, k - 1)) + (
                    at(v_ext, base[0] + 2, k) - at(v_ext, base[0] + 2, k, -1)
                )
            s_ext[f, k, pl.ds(begin, rows), :] = relax * at(s_ext, f, k) + shear * strain

    def there(step, f, d):
        t = lax.rem(me + d, n)
        ys, xs = piece(t)
        src = acc.at[f, :, ys, xs]
        dst = pin.at[f, pl.ds(me * depth, depth)]
        if d == 0:
            return pltpu.make_async_copy(src, dst, f_recv.at[step, f, 0])
        return pltpu.make_async_remote_copy(
            src_ref=src, dst_ref=dst, send_sem=f_send.at[step, f, d],
            recv_sem=f_recv.at[step, f, d], device_id=(t, g), device_id_type=MESH,
        )

    def back(step, f, d):
        t = lax.rem(me + d, n)
        ys, xs = pl.ds(pl.multiple_of((me // tiles) * ROWS + ROWS, ROWS), ROWS), piece(me)[1]
        last = step == STEPS - 1
        low, count = (1 if last and f == 2 else 0), depth + (1 if last else 2)
        src = pout.at[f, pl.ds(t * depth + low, count)]
        dst = v_ext.at[3 * step + f, pl.ds(low, count), ys, xs]
        if d == 0:
            return pltpu.make_async_copy(src, dst, r_recv.at[step, f, 0])
        return pltpu.make_async_remote_copy(
            src_ref=src, dst_ref=dst, send_sem=r_send.at[step, f, d],
            recv_sem=r_recv.at[step, f, d], device_id=(t, g), device_id_type=MESH,
        )

    def start_all(make, step, f):
        for d in list(range(1, n)) + [0]:
            make(step, f, d).start()

    def wait_sent(make, step, f):
        for d in range(1, n):
            make(step, f, d).wait_send()

    def wait_got(make, step, f):
        make(step, f, 0).wait()
        for d in range(1, n):
            make(step, f, d).wait_recv()

    def share(step, d):
        return pltpu.make_async_remote_copy(
            src_ref=um.at[step, 0], dst_ref=um.at[step, d],
            send_sem=u_send.at[step, d], recv_sem=u_recv.at[step, d],
            device_id=(me, lax.rem(g + d, ng)), device_id_type=MESH,
        )

    def y_speed(step, f, i):
        return pltpu.make_async_remote_copy(
            src_ref=yg_send.at[step, f, i], dst_ref=yg_recv.at[step, f, i],
            send_sem=y_send.at[step, f, i], recv_sem=y_recv.at[step, f, i],
            device_id=(me, g + 1 - 2 * i), device_id_type=MESH,
        )

    has_next, has_last = g < ng - 1, g > 0
    planes = pl.ds(0, depth + 2)

    def stress_xy():
        def at(i, carry):
            shears(i + 1, ROWS, ROWS + side, (3,))
            return carry

        lax.fori_loop(0, depth, at, 0)

        @pl.when(g == ng - 1)
        def _():
            s_ext[3, planes, ROWS + side, :] = jnp.zeros((depth + 2, line), jnp.float32)

    def stress_xz():
        def at(i, carry):
            normals(i + 1, ROWS, side, (0,))
            shears(i + 1, ROWS, side, (4,))
            return carry

        lax.fori_loop(0, depth, at, 0)
        shears(depth + 1, ROWS, side, (4,))

    def stress_yz():
        def at(i, carry):
            normals(i + 1, 0, ROWS + side, (1,))
            shears(i + 1, ROWS, ROWS + side, (5,))
            return carry

        lax.fori_loop(0, depth, at, 0)
        shears(depth + 1, ROWS, side, (5,))

        @pl.when(g == 0)
        def _():
            s_ext[1, planes, ROWS - 1, :] = jnp.zeros((depth + 2, line), jnp.float32)

        @pl.when(g == ng - 1)
        def _():
            s_ext[5, planes, ROWS + side, :] = jnp.zeros((depth + 2, line), jnp.float32)

    def stress_zz():
        def at(i, carry):
            normals(i, ROWS, side, (2,))
            return carry

        lax.fori_loop(0, depth + 1, at, 0)

    def v_copy(f):
        return pltpu.make_async_copy(
            v_ext.at[3 * (STEPS - 1) + f, pl.ds(1, depth), inner, :], v_out.at[f], o_sem.at[f]
        )

    def out_copy(f):
        return pltpu.make_async_copy(
            s_ext.at[f, pl.ds(1, depth), inner, :], s_out.at[f], o_sem.at[3 + f]
        )

    def arrive(f, step):
        wait_got(back, step, f)
        yg_send[step, f, 0] = v_ext[3 * step + f, planes, ROWS + side - 1, :]
        yg_send[step, f, 1] = v_ext[3 * step + f, planes, ROWS, :]

        @pl.when(has_next)
        def _():
            y_speed(step, f, 0).start()

        @pl.when(has_last)
        def _():
            y_speed(step, f, 1).start()
        if step == STEPS - 1:
            v_copy(f).start()

    def edges(f, step):
        @pl.when(has_last)
        def _():
            y_speed(step, f, 0).wait_recv()
            v_ext[3 * step + f, planes, ROWS - 1, :] = yg_recv[step, f, 0]
            y_speed(step, f, 1).wait_send()

        @pl.when(has_next)
        def _():
            y_speed(step, f, 1).wait_recv()
            v_ext[3 * step + f, planes, ROWS + side, :] = yg_recv[step, f, 1]
            y_speed(step, f, 0).wait_send()

    for step in range(STEPS):
        if step > 0:
            for f in range(3):
                wait_sent(there, step - 1, f)
        if step > 0:
            stress_xz()
        lax.fori_loop(0, depth, speed_x, 0)
        start_all(there, step, 0)
        if step > 0:
            edges(2, step - 1)
            stress_yz()
        lax.fori_loop(0, depth, speed_y, 0)
        start_all(there, step, 1)
        if step > 0:
            stress_zz()
        lax.fori_loop(0, depth, speed_z, 0)
        flat = acc[2].reshape(depth * side, line)
        part = lax.dot_general(
            flat, in_cols, (((1,), (1,)), ((), ())),
            precision=lax.Precision.HIGHEST, preferred_element_type=jnp.float32,
        ).reshape(depth, side, LANES)
        um[step, 0, pl.ds(0, depth), :] = jnp.sum(part * in_rows[None], axis=1)
        um[step, 0, pl.ds(depth, depth), :] = w_ref[...]
        um[step, 0, pl.ds(2 * depth, ROWS), :] = imp_ref[...]
        for d in range(1, ng):
            share(step, d).start()
        for d in range(1, ng):
            share(step, d).wait()
        every = um[step, 0]
        for d in range(1, ng):
            every = every + um[step, d]
        w = every[depth : 2 * depth] if step == 0 else wbuf[...]
        force = every[2 * depth : 2 * depth + 1] * (w - every[0:depth] / FOOT)
        wbuf[...] = w - pier_gain * force
        spread = (force[:, None, :] * in_rows[None]).reshape(depth * side, LANES)
        pushed = jnp.dot(
            spread, in_cols, precision=lax.Precision.HIGHEST, preferred_element_type=jnp.float32
        )
        acc[2] = acc[2] + soil_gain * pushed.reshape(depth, side, line)
        start_all(there, step, 2)

        for f in range(3):
            wait_got(there, step, f)
            if step > 0:
                wait_sent(back, step - 1, f)
            full = jnp.concatenate([pin[f, :, y, :] for y in range(ROWS)], axis=1)
            damped = jnp.dot(
                damp_ref[...], full, precision=lax.Precision.HIGHEST,
                preferred_element_type=jnp.float32,
            )
            for y in range(ROWS):
                pout[f, pl.ds(1, n * depth), y, :] = damped[:, y * LANES : (y + 1) * LANES]
            start_all(back, step, f)
        base[0] = 3 * step
        arrive(0, step)
        arrive(1, step)
        edges(0, step)
        edges(1, step)
        if step < STEPS - 1:
            stress_xy()
            arrive(2, step)
        else:
            def last_xy(i, carry):
                shears(i + 1, ROWS, side, (3,))
                return carry

            def last_rest(i, carry):
                normals(i + 1, ROWS, side)
                shears(i + 1, ROWS, side, (4,))
                return carry

            def last_yz(i, carry):
                shears(i + 1, ROWS, side, (5,))
                return carry

            lax.fori_loop(0, depth, last_xy, 0)
            out_copy(3).start()
            arrive(2, step)
            lax.fori_loop(0, depth, last_rest, 0)
            for f in (0, 1, 2, 4):
                out_copy(f).start()
            edges(2, step)
            lax.fori_loop(0, depth, last_yz, 0)
            out_copy(5).start()

    w_out[...] = wbuf[...]
    for f in range(3):
        wait_sent(there, STEPS - 1, f)
        wait_sent(back, STEPS - 1, f)
    for f in range(3):
        v_copy(f).wait()
    for f in range(6):
        out_copy(f).wait()


def fused_body(
    n, ng, velocity, stress, pier_velocity, buoyancy, layer, lame_table, shear_table, relax_table,
    impedance, footprint, damp_inverse,
):
    depth, side, line = buoyancy.shape
    own = pier_velocity.shape[1]
    piers = footprint.shape[0]
    g = lax.axis_index("gy")
    lane = jnp.arange(LANES, dtype=jnp.int32)
    w_all = lax.dynamic_update_slice(
        jnp.zeros((depth, LANES), jnp.float32), pier_velocity, (0, g * own)
    )
    imp = lax.dynamic_update_slice(
        jnp.zeros((ROWS, LANES), jnp.float32),
        jnp.broadcast_to(impedance[None, :], (ROWS, own)), (0, g * own)
    )
    corner = jnp.pad(footprint[:, 0], (0, LANES - piers), constant_values=-line * 64)
    rows = jnp.broadcast_to((corner // line)[None, :], (ROWS, LANES))
    cols = jnp.where(lane < piers, corner % line, -64)
    cols = jnp.broadcast_to(cols[:, None], (LANES, LANES))
    f32 = jnp.float32
    hbm = pl.BlockSpec(memory_space=pl.ANY)
    vmem = pl.BlockSpec(memory_space=pltpu.VMEM)
    smem = pl.BlockSpec(memory_space=pltpu.SMEM)
    dma = pltpu.SemaphoreType.DMA
    tall = side + 2 * ROWS
    stage = 2 * depth + ROWS
    v, s, w = pl.pallas_call(
        functools.partial(fused, n, ng),
        out_shape=(
            jax.ShapeDtypeStruct(velocity.shape, f32),
            jax.ShapeDtypeStruct(stress.shape, f32),
            jax.ShapeDtypeStruct((depth, LANES), f32),
        ),
        in_specs=[hbm] * 3 + [smem] * 4 + [vmem] * 5,
        out_specs=(hbm, hbm, vmem),
        scratch_shapes=[
            pltpu.VMEM((3 * STEPS, depth + 2, tall, line), f32),
            pltpu.VMEM((6, depth + 2, tall, line), f32),
            pltpu.VMEM((depth, side, line), f32),
            pltpu.VMEM((3, depth + 2, ROWS, LANES), f32),
            pltpu.VMEM((3, depth, side, line), f32),
            pltpu.VMEM((3, n * depth, ROWS, LANES), f32),
            pltpu.VMEM((3, n * depth + 2, ROWS, LANES), f32),
            pltpu.VMEM((STEPS, ng, stage, LANES), f32),
            pltpu.VMEM((depth, LANES), f32),
            pltpu.VMEM((3, depth, line), f32),
            pltpu.VMEM((3, depth, line), f32),
            pltpu.VMEM((STEPS, 3, 2, depth + 2, line), f32),
            pltpu.VMEM((STEPS, 3, 2, depth + 2, line), f32),
            dma((10,)), dma((3,)), dma((3,)), dma((2,)), dma((2,)), dma((3,)), dma((3,)),
            dma((STEPS, 3, n)), dma((STEPS, 3, n)), dma((STEPS, 3, n)), dma((STEPS, 3, n)),
            dma((STEPS, ng)), dma((STEPS, ng)), dma((STEPS, 3, 2)), dma((STEPS, 3, 2)),
            dma((9,)),
        ],
        compiler_params=pltpu.CompilerParams(
            collective_id=0, has_side_effects=True, vmem_limit_bytes=60 * 1024 * 1024
        ),
    )(
        velocity, stress, buoyancy, layer, lame_table, shear_table, relax_table,
        w_all, imp, rows, cols, damp_inverse,
    )
    return v, s, lax.dynamic_slice(w, (0, g * own), (depth, own))


def whole_tiles(mesh, velocity, pier_velocity):
    n, ng = mesh.shape["gx"], mesh.shape["gy"]
    depth, side, line = velocity.shape[1] // n, velocity.shape[2] // ng, velocity.shape[3]
    return (
        line % LANES == 0
        and side % ROWS == 0
        and depth % ROWS == 0
        and (side // ROWS) * (line // LANES) == n
        and pier_velocity.shape[1] <= LANES
    )


def solution(mesh):
    placed = (
        P(None, "gx", "gy", None),
        P(None, "gx", "gy", None),
        P("gx", "gy"),
        P("gx", "gy", None),
        P("gx"),
        P(),
        P(),
        P(),
        P("gy"),
        P(),
        P(),
    )

    def run(*args):
        n, ng = mesh.shape["gx"], mesh.shape["gy"]
        if whole_tiles(mesh, args[0], args[2]):
            part = functools.partial(fused_body, n, ng)
        else:
            part = body
        return mapped(part)(*args)

    def mapped(part):
        return jax.shard_map(
            part,
            mesh=mesh,
            in_specs=placed,
            out_specs=(P(None, "gx", "gy", None), P(None, "gx", "gy", None), P("gx", "gy")),
            check_vma=False,
        )

    return run
```

```python
import functools
import jax
import jax.numpy as jnp
from jax import lax
from jax.experimental import pallas as pl
from jax.experimental.pallas import tpu as pltpu
from jax.sharding import PartitionSpec as P

STEPS = 2
FOOT = 16


grid_ratio = 0.25
soil_gain = 0.2
pier_gain = 0.5


def extended(cells, sides, width):
    for axis, dim in sides:
        count = lax.axis_size(axis)
        ends = count - 1
        head = lax.slice_in_dim(cells, 0, width, axis=dim)
        tail = lax.slice_in_dim(cells, cells.shape[dim] - width, cells.shape[dim], axis=dim)
        cells = jnp.concatenate(
            [
                lax.ppermute(tail, axis, [(i, (i + 1) % count) for i in range(ends)]),
                cells,
                lax.ppermute(head, axis, [((i + 1) % count, i) for i in range(ends)]),
            ],
            axis=dim,
        )
    return cells


def forward_diff(padded, along):
    center = padded[1:-1, 1:-1, 1:-1]
    if along == 0:
        return padded[2:, 1:-1, 1:-1] - center
    if along == 1:
        return padded[1:-1, 2:, 1:-1] - center
    return padded[1:-1, 1:-1, 2:] - center


def backward_diff(padded, along):
    center = padded[1:-1, 1:-1, 1:-1]
    if along == 0:
        return center - padded[:-2, 1:-1, 1:-1]
    if along == 1:
        return center - padded[1:-1, :-2, 1:-1]
    return center - padded[1:-1, 1:-1, :-2]


def move_velocity(velocity, padded, buoyancy):
    scaled = grid_ratio * buoyancy
    first = velocity[0] + scaled * (
        backward_diff(padded[0], 2) + forward_diff(padded[3], 1) + forward_diff(padded[4], 0)
    )
    second = velocity[1] + scaled * (
        forward_diff(padded[3], 2) + backward_diff(padded[1], 1) + forward_diff(padded[5], 0)
    )
    third = velocity[2] + scaled * (
        forward_diff(padded[4], 2) + forward_diff(padded[5], 1) + backward_diff(padded[2], 0)
    )
    return jnp.stack([first, second, third])


def move_stress(stress, padded, lame_first, shear_mod, relax):
    strain_x = forward_diff(padded[0], 2)
    strain_y = forward_diff(padded[1], 1)
    strain_z = forward_diff(padded[2], 0)
    modulus = lame_first + 2.0 * shear_mod
    normal_x = relax * stress[0] + grid_ratio * (
        modulus * strain_x + lame_first * (strain_y + strain_z)
    )
    normal_y = relax * stress[1] + grid_ratio * (
        modulus * strain_y + lame_first * (strain_x + strain_z)
    )
    normal_z = relax * stress[2] + grid_ratio * (
        modulus * strain_z + lame_first * (strain_x + strain_y)
    )
    shear_xy = relax * stress[3] + grid_ratio * shear_mod * (
        backward_diff(padded[0], 1) + backward_diff(padded[1], 2)
    )
    shear_xz = relax * stress[4] + grid_ratio * shear_mod * (
        backward_diff(padded[0], 0) + backward_diff(padded[2], 2)
    )
    shear_yz = relax * stress[5] + grid_ratio * shear_mod * (
        backward_diff(padded[1], 0) + backward_diff(padded[2], 1)
    )
    return jnp.stack([normal_x, normal_y, normal_z, shear_xy, shear_xz, shear_yz])


def layer_values(layer, table):
    levels = jnp.arange(table.shape[0], dtype=jnp.int32)
    onehot = (layer[:, None] == levels[None, :]).astype(table.dtype)
    return jnp.sum(onehot * table[None, :], axis=1)[:, None, None]


def with_faces(fields):
    padded = extended(fields, (("gx", 1), ("gy", 2)), 1)
    return jnp.pad(padded, ((0, 0), (0, 0), (0, 0), (1, 1)))


def footprint_matches(cell_ids, footprint):
    piers = footprint.shape[0]
    equal = (cell_ids[:, None] == footprint.reshape(-1)[None, :]).astype(jnp.float32)
    return jnp.sum(equal.reshape(cell_ids.shape[0], piers, FOOT), axis=2)


def damp_columns(velocity, inverse):
    pencils = lax.all_to_all(velocity, "gx", split_axis=3, concat_axis=1, tiled=True)
    shape = pencils.shape
    flat = pencils.reshape(shape[0], shape[1], shape[2] * shape[3])
    damped = jnp.einsum("zk,fkm->fzm", inverse, flat, precision=lax.Precision.HIGHEST).reshape(
        shape
    )
    return lax.all_to_all(damped, "gx", split_axis=1, concat_axis=3, tiled=True)


def body(
    velocity,
    stress,
    pier_velocity,
    buoyancy,
    layer,
    lame_table,
    shear_table,
    relax_table,
    impedance,
    footprint,
    damp_inverse,
):
    depth_cells, side_cells, line_cells = (velocity.shape[1], velocity.shape[2], velocity.shape[3])
    own_piers = pier_velocity.shape[1]
    lame_first = layer_values(layer, lame_table)
    shear_mod = layer_values(layer, shear_table)
    relax = layer_values(layer, relax_table)
    row_start = lax.axis_index("gy") * side_cells
    cell_ids = row_start * line_cells + jnp.arange(side_cells * line_cells, dtype=jnp.int32)
    selector = footprint_matches(cell_ids, footprint)
    own_foot = lax.dynamic_slice_in_dim(footprint, lax.axis_index("gy") * own_piers, own_piers, 0)
    for time_step in range(STEPS):
        padded = with_faces(stress)
        velocity = move_velocity(velocity, padded, buoyancy)
        vertical = velocity[2].reshape(depth_cells, side_cells * line_cells)
        piece = lax.all_gather(velocity[2], "gy", axis=1, tiled=True)
        count = piece.shape[1]
        piece_ids = jnp.arange(count * line_cells, dtype=jnp.int32)
        picks = footprint_matches(piece_ids, own_foot)
        flat = piece.reshape(depth_cells, count * line_cells)
        summed = jnp.dot(
            flat, picks, precision=lax.Precision.HIGHEST, preferred_element_type=jnp.float32
        )
        mean_speed = summed / FOOT
        force = impedance[None, :] * (pier_velocity - mean_speed)
        pier_velocity = pier_velocity - pier_gain * force
        all_force = lax.all_gather(force, "gy", axis=1, tiled=True)
        pushed = jnp.dot(
            all_force,
            selector.T,
            precision=lax.Precision.HIGHEST,
            preferred_element_type=jnp.float32,
        )
        vertical = vertical + soil_gain * pushed
        velocity = jnp.stack(
            [velocity[0], velocity[1], vertical.reshape(depth_cells, side_cells, line_cells)]
        )
        velocity = damp_columns(velocity, damp_inverse)
        padded = with_faces(velocity)
        stress = move_stress(stress, padded, lame_first, shear_mod, relax)
    return (velocity, stress, pier_velocity)


SIDE = 4
LANES = 128
ROWS = 8
MESH = pl.DeviceIdType.MESH
Z_GHOSTS = ((2, -1), (4, 1), (5, 1))
Y_GHOSTS = ((1, -1), (3, 1), (5, 1))


def shift_x(a, ahead):
    lane = lax.broadcasted_iota(jnp.int32, a.shape, 1)
    width = a.shape[1]
    if ahead:
        return jnp.where(lane == width - 1, 0.0, pltpu.roll(a, width - 1, 1))
    return jnp.where(lane == 0, 0.0, pltpu.roll(a, 1, 1))


def fused(
    n, ng, v_hbm, s_hbm, b_hbm, layer_ref, lame_ref, shear_ref, relax_ref, foot_ref, w_ref, imp_ref, damp_ref,
    v_out, s_out, w_out,
    v_ext, s_ext, buoy, coef, acc, pin, pout, um, wbuf, sg_send, sg_recv, yg_send, yg_recv,
    load_sem, zs_send, zs_recv, cf_send, cf_recv, ys_send, ys_recv,
    f_send, f_recv, r_send, r_recv, u_send, u_recv, y_send, y_recv, o_sem,
):
    me = lax.axis_index("gx")
    g = lax.axis_index("gy")
    depth, side, line = buoy.shape
    tiles = line // LANES
    inner = pl.ds(ROWS, side)

    def piece(j):
        return (
            pl.ds(pl.multiple_of((j // tiles) * ROWS, ROWS), ROWS),
            pl.ds(pl.multiple_of((j % tiles) * LANES, LANES), LANES),
        )

    loads = {}
    for slot, f in enumerate((1, 3, 5, 2, 4, 0)):
        loads[("s", f)] = pltpu.make_async_copy(
            s_hbm.at[f], s_ext.at[f, pl.ds(1, depth), inner, :], load_sem.at[slot]
        )
    loads["b"] = pltpu.make_async_copy(b_hbm, buoy, load_sem.at[6])
    for f in range(3):
        loads[("v", f)] = pltpu.make_async_copy(
            v_hbm.at[f], v_ext.at[f, pl.ds(1, depth), inner, :], load_sem.at[7 + f]
        )
    for copy in loads.values():
        copy.start()

    plane = jnp.zeros((side, line), jnp.float32)
    for f, way in Z_GHOSTS:
        s_ext[f, 0 if way < 0 else depth + 1, inner, :] = plane
    edge = jnp.zeros((ROWS, line), jnp.float32)

    def clear(k, carry):
        for f, way in Y_GHOSTS:
            s_ext[f, k, pl.ds(0 if way < 0 else ROWS + side, ROWS), :] = edge
        for f in range(3 * STEPS):
            v_ext[f, k, pl.ds(0, ROWS), :] = edge
            v_ext[f, k, pl.ds(ROWS + side, ROWS), :] = edge
        return carry

    lax.fori_loop(0, depth + 2, clear, 0)
    for k in range(depth):
        for c, table in enumerate((lame_ref, shear_ref, relax_ref)):
            coef[c, k + 1] = jnp.full((ROWS, LANES), table[layer_ref[k]], jnp.float32)
    for c in range(3):
        coef[c, 0] = jnp.zeros((ROWS, LANES), jnp.float32)
        coef[c, depth + 1] = jnp.zeros((ROWS, LANES), jnp.float32)
        pout[c, 0] = jnp.zeros((ROWS, LANES), jnp.float32)
        pout[c, n * depth + 1] = jnp.zeros((ROWS, LANES), jnp.float32)

    barrier = pltpu.get_barrier_semaphore()
    for d in range(1, n):
        pl.semaphore_signal(
            barrier, inc=1, device_id=(lax.rem(me + d, n), g), device_id_type=MESH
        )
    for d in range(1, ng):
        pl.semaphore_signal(
            barrier, inc=1, device_id=(me, lax.rem(g + d, ng)), device_id_type=MESH
        )
    pl.semaphore_wait(barrier, n - 1 + ng - 1)

    def z_copy(i):
        f, way = Z_GHOSTS[i]
        return pltpu.make_async_remote_copy(
            src_ref=s_hbm.at[f, depth - 1 if way < 0 else 0],
            dst_ref=s_ext.at[f, 0 if way < 0 else depth + 1, inner, :],
            send_sem=zs_send.at[i],
            recv_sem=zs_recv.at[i],
            device_id=(me - way, g),
            device_id_type=MESH,
        )

    def c_copy(way):
        i = (way + 1) // 2
        return pltpu.make_async_remote_copy(
            src_ref=coef.at[:, depth if way < 0 else 1],
            dst_ref=coef.at[:, 0 if way < 0 else depth + 1],
            send_sem=cf_send.at[i],
            recv_sem=cf_recv.at[i],
            device_id=(me - way, g),
            device_id_type=MESH,
        )

    def y_stress(i):
        f, way = Y_GHOSTS[i]
        return pltpu.make_async_remote_copy(
            src_ref=sg_send.at[i],
            dst_ref=sg_recv.at[i],
            send_sem=ys_send.at[i],
            recv_sem=ys_recv.at[i],
            device_id=(me, g - way),
            device_id_type=MESH,
        )

    not_ends = {
        -1: (me > 0, me < n - 1, g > 0, g < ng - 1),
        1: (me < n - 1, me > 0, g < ng - 1, g > 0),
    }

    for i, (f, way) in enumerate(Z_GHOSTS):
        @pl.when(not_ends[way][1])
        def _(i=i):
            z_copy(i).start()
    for way in (-1, 1):
        @pl.when(not_ends[way][1])
        def _(way=way):
            c_copy(way).start()
    for i, (f, way) in enumerate(Y_GHOSTS):
        loads[("s", f)].wait()
        sg_send[i] = s_ext[f, pl.ds(1, depth), ROWS + side - 1 if way < 0 else ROWS, :]

        @pl.when(not_ends[way][3])
        def _(i=i):
            y_stress(i).start()
    for key, copy in loads.items():
        if key not in (("s", 1), ("s", 3), ("s", 5)):
            copy.wait()

    ids = lax.broadcasted_iota(jnp.int32, (side, LANES), 0) + g * side
    by_lane = lax.broadcasted_iota(jnp.int32, (side, LANES), 1)
    by_row = lax.broadcasted_iota(jnp.int32, (LANES, LANES), 0)
    first = jnp.full((side, LANES), -64, jnp.int32)
    begin = jnp.full((LANES, LANES), -64, jnp.int32)
    for p in range(foot_ref.shape[0]):
        first = jnp.where(by_lane == p, foot_ref[p, 0] // line, first)
        begin = jnp.where(by_row == p, foot_ref[p, 0] % line, begin)
    in_rows = jnp.where((ids >= first) & (ids < first + SIDE), 1.0, 0.0)
    across = lax.broadcasted_iota(jnp.int32, (LANES, line), 1)
    start = jnp.concatenate([begin] * tiles, axis=1)
    in_cols = jnp.where((across >= start) & (across < start + SIDE), 1.0, 0.0)

    for i, (f, way) in enumerate(Z_GHOSTS):
        @pl.when(not_ends[way][0])
        def _(i=i):
            z_copy(i).wait_recv()

        @pl.when(not_ends[way][1])
        def _(i=i):
            z_copy(i).wait_send()
    for way in (-1, 1):
        @pl.when(not_ends[way][0])
        def _(way=way):
            c_copy(way).wait_recv()

        @pl.when(not_ends[way][1])
        def _(way=way):
            c_copy(way).wait_send()
    for i, (f, way) in enumerate(Y_GHOSTS):
        @pl.when(not_ends[way][2])
        def _(i=i, f=f, way=way):
            y_stress(i).wait_recv()
            s_ext[f, pl.ds(1, depth), ROWS - 1 if way < 0 else ROWS + side, :] = sg_recv[i]

        @pl.when(not_ends[way][3])
        def _(i=i):
            y_stress(i).wait_send()

    def cells(ref, f, k, shift=0, begin=ROWS, rows=None):
        return ref[f, k, pl.ds(begin + shift, side if rows is None else rows), :]

    base = [0]

    def speed_x(i, carry):
        k = i + 1
        xx, xy, xz = cells(s_ext, 0, k), cells(s_ext, 3, k), cells(s_ext, 4, k)
        total = (xx - shift_x(xx, False)) + (cells(s_ext, 3, k, 1) - xy)
        total = total + (cells(s_ext, 4, k + 1) - xz)
        acc[0, i] = cells(v_ext, base[0] + 0, k) + (grid_ratio * buoy[i]) * total
        return carry

    def speed_y(i, carry):
        k = i + 1
        xy, yy, yz = cells(s_ext, 3, k), cells(s_ext, 1, k), cells(s_ext, 5, k)
        total = (shift_x(xy, True) - xy) + (yy - cells(s_ext, 1, k, -1))
        total = total + (cells(s_ext, 5, k + 1) - yz)
        acc[1, i] = cells(v_ext, base[0] + 1, k) + (grid_ratio * buoy[i]) * total
        return carry

    def speed_z(i, carry):
        k = i + 1
        xz, yz, zz = cells(s_ext, 4, k), cells(s_ext, 5, k), cells(s_ext, 2, k)
        total = (shift_x(xz, True) - xz) + (cells(s_ext, 5, k, 1) - yz)
        total = total + (zz - cells(s_ext, 2, k - 1))
        acc[2, i] = cells(v_ext, base[0] + 2, k) + (grid_ratio * buoy[i]) * total
        return carry

    def wide(c, k, rows):
        tile = jnp.concatenate([coef[c, k]] * tiles, axis=1)
        return jnp.concatenate([tile] * (rows // ROWS), axis=0)

    def normals(k, begin, rows, which=(0, 1, 2)):
        at = functools.partial(cells, begin=begin, rows=rows)
        lame, shear, relax = (wide(c, k, rows) for c in range(3))
        vx, vy, vz = at(v_ext, base[0] + 0, k), at(v_ext, base[0] + 1, k), at(v_ext, base[0] + 2, k)
        ex = shift_x(vx, True) - vx
        ey = at(v_ext, base[0] + 1, k, 1) - vy
        ez = at(v_ext, base[0] + 2, k + 1) - vz
        modulus = lame + 2.0 * shear
        for f in which:
            own, others = ((ex, ey + ez), (ey, ex + ez), (ez, ex + ey))[f]
            s_ext[f, k, pl.ds(begin, rows), :] = relax * at(s_ext, f, k) + grid_ratio * (
                modulus * own + lame * others
            )

    def shears(k, begin, rows, which):
        at = functools.partial(cells, begin=begin, rows=rows)
        shear, relax = grid_ratio * wide(1, k, rows), wide(2, k, rows)
        for f in which:
            if f == 3:
                vy = at(v_ext, base[0] + 1, k)
                strain = (at(v_ext, base[0] + 0, k) - at(v_ext, base[0] + 0, k, -1)) + (vy - shift_x(vy, False))
            elif f == 4:
                vz = at(v_ext, base[0] + 2, k)
                strain = (at(v_ext, base[0] + 0, k) - at(v_ext, base[0] + 0, k - 1)) + (vz - shift_x(vz, False))
            else:
                strain = (at(v_ext, base[0] + 1, k) - at(v_ext, base[0] + 1, k - 1)) + (
                    at(v_ext, base[0] + 2, k) - at(v_ext, base[0] + 2, k, -1)
                )
            s_ext[f, k, pl.ds(begin, rows), :] = relax * at(s_ext, f, k) + shear * strain

    def there(step, f, d):
        t = lax.rem(me + d, n)
        ys, xs = piece(t)
        src = acc.at[f, :, ys, xs]
        dst = pin.at[f, pl.ds(me * depth, depth)]
        if d == 0:
            return pltpu.make_async_copy(src, dst, f_recv.at[step, f, 0])
        return pltpu.make_async_remote_copy(
            src_ref=src, dst_ref=dst, send_sem=f_send.at[step, f, d],
            recv_sem=f_recv.at[step, f, d], device_id=(t, g), device_id_type=MESH,
        )

    def back(step, f, d):
        t = lax.rem(me + d, n)
        ys, xs = pl.ds(pl.multiple_of((me // tiles) * ROWS + ROWS, ROWS), ROWS), piece(me)[1]
        last = step == STEPS - 1
        low, count = (1 if last and f == 2 else 0), depth + (1 if last else 2)
        src = pout.at[f, pl.ds(t * depth + low, count)]
        dst = v_ext.at[3 * step + f, pl.ds(low, count), ys, xs]
        if d == 0:
            return pltpu.make_async_copy(src, dst, r_recv.at[step, f, 0])
        return pltpu.make_async_remote_copy(
            src_ref=src, dst_ref=dst, send_sem=r_send.at[step, f, d],
            recv_sem=r_recv.at[step, f, d], device_id=(t, g), device_id_type=MESH,
        )

    def start_all(make, step, f):
        for d in list(range(1, n)) + [0]:
            make(step, f, d).start()

    def wait_sent(make, step, f):
        for d in range(1, n):
            make(step, f, d).wait_send()

    def wait_got(make, step, f):
        make(step, f, 0).wait()
        for d in range(1, n):
            make(step, f, d).wait_recv()

    def share(step, d):
        return pltpu.make_async_remote_copy(
            src_ref=um.at[step, 0], dst_ref=um.at[step, d],
            send_sem=u_send.at[step, d], recv_sem=u_recv.at[step, d],
            device_id=(me, lax.rem(g + d, ng)), device_id_type=MESH,
        )

    def y_speed(step, f, i):
        return pltpu.make_async_remote_copy(
            src_ref=yg_send.at[step, f, i], dst_ref=yg_recv.at[step, f, i],
            send_sem=y_send.at[step, f, i], recv_sem=y_recv.at[step, f, i],
            device_id=(me, g + 1 - 2 * i), device_id_type=MESH,
        )

    has_next, has_last = g < ng - 1, g > 0
    planes = pl.ds(0, depth + 2)

    def stress_xy():
        def at(i, carry):
            shears(i + 1, ROWS, ROWS + side, (3,))
            return carry

        lax.fori_loop(0, depth, at, 0)

        @pl.when(g == ng - 1)
        def _():
            s_ext[3, planes, ROWS + side, :] = jnp.zeros((depth + 2, line), jnp.float32)

    def stress_xz():
        def at(i, carry):
            normals(i + 1, ROWS, side, (0,))
            shears(i + 1, ROWS, side, (4,))
            return carry

        lax.fori_loop(0, depth, at, 0)
        shears(depth + 1, ROWS, side, (4,))

    def stress_yz():
        def at(i, carry):
            normals(i + 1, 0, ROWS + side, (1,))
            shears(i + 1, ROWS, ROWS + side, (5,))
            return carry

        lax.fori_loop(0, depth, at, 0)
        shears(depth + 1, ROWS, side, (5,))

        @pl.when(g == 0)
        def _():
            s_ext[1, planes, ROWS - 1, :] = jnp.zeros((depth + 2, line), jnp.float32)

        @pl.when(g == ng - 1)
        def _():
            s_ext[5, planes, ROWS + side, :] = jnp.zeros((depth + 2, line), jnp.float32)

    def stress_zz():
        def at(i, carry):
            normals(i, ROWS, side, (2,))
            return carry

        lax.fori_loop(0, depth + 1, at, 0)

    def v_copy(f):
        return pltpu.make_async_copy(
            v_ext.at[3 * (STEPS - 1) + f, pl.ds(1, depth), inner, :], v_out.at[f], o_sem.at[f]
        )

    def out_copy(f):
        return pltpu.make_async_copy(
            s_ext.at[f, pl.ds(1, depth), inner, :], s_out.at[f], o_sem.at[3 + f]
        )

    def arrive(f, step):
        wait_got(back, step, f)
        yg_send[step, f, 0] = v_ext[3 * step + f, planes, ROWS + side - 1, :]
        yg_send[step, f, 1] = v_ext[3 * step + f, planes, ROWS, :]

        @pl.when(has_next)
        def _():
            y_speed(step, f, 0).start()

        @pl.when(has_last)
        def _():
            y_speed(step, f, 1).start()
        if step == STEPS - 1:
            v_copy(f).start()

    def edges(f, step):
        @pl.when(has_last)
        def _():
            y_speed(step, f, 0).wait_recv()
            v_ext[3 * step + f, planes, ROWS - 1, :] = yg_recv[step, f, 0]
            y_speed(step, f, 1).wait_send()

        @pl.when(has_next)
        def _():
            y_speed(step, f, 1).wait_recv()
            v_ext[3 * step + f, planes, ROWS + side, :] = yg_recv[step, f, 1]
            y_speed(step, f, 0).wait_send()

    for step in range(STEPS):
        if step > 0:
            for f in range(3):
                wait_sent(there, step - 1, f)
        if step > 0:
            stress_xz()
        lax.fori_loop(0, depth, speed_x, 0)
        start_all(there, step, 0)
        if step > 0:
            edges(2, step - 1)
            stress_yz()
        lax.fori_loop(0, depth, speed_y, 0)
        start_all(there, step, 1)
        if step > 0:
            stress_zz()
        lax.fori_loop(0, depth, speed_z, 0)
        flat = acc[2].reshape(depth * side, line)
        part = lax.dot_general(
            flat, in_cols, (((1,), (1,)), ((), ())),
            precision=lax.Precision.HIGHEST, preferred_element_type=jnp.float32,
        ).reshape(depth, side, LANES)
        um[step, 0, pl.ds(0, depth), :] = jnp.sum(part * in_rows[None], axis=1)
        um[step, 0, pl.ds(depth, depth), :] = w_ref[...]
        um[step, 0, pl.ds(2 * depth, ROWS), :] = imp_ref[...]
        for d in range(1, ng):
            share(step, d).start()
        for d in range(1, ng):
            share(step, d).wait()
        every = um[step, 0]
        for d in range(1, ng):
            every = every + um[step, d]
        w = every[depth : 2 * depth] if step == 0 else wbuf[...]
        force = every[2 * depth : 2 * depth + 1] * (w - every[0:depth] / FOOT)
        wbuf[...] = w - pier_gain * force
        spread = (force[:, None, :] * in_rows[None]).reshape(depth * side, LANES)
        pushed = jnp.dot(
            spread, in_cols, precision=lax.Precision.HIGHEST, preferred_element_type=jnp.float32
        )
        acc[2] = acc[2] + soil_gain * pushed.reshape(depth, side, line)
        start_all(there, step, 2)

        for f in range(3):
            wait_got(there, step, f)
            if step > 0:
                wait_sent(back, step - 1, f)
            full = jnp.concatenate([pin[f, :, y, :] for y in range(ROWS)], axis=1)
            damped = jnp.dot(
                damp_ref[...], full, precision=lax.Precision.HIGHEST,
                preferred_element_type=jnp.float32,
            )
            for y in range(ROWS):
                pout[f, pl.ds(1, n * depth), y, :] = damped[:, y * LANES : (y + 1) * LANES]
            start_all(back, step, f)
        base[0] = 3 * step
        arrive(0, step)
        arrive(1, step)
        edges(0, step)
        edges(1, step)
        if step < STEPS - 1:
            stress_xy()
            arrive(2, step)
        else:
            def last_xy(i, carry):
                shears(i + 1, ROWS, side, (3,))
                return carry

            def last_rest(i, carry):
                normals(i + 1, ROWS, side)
                shears(i + 1, ROWS, side, (4,))
                return carry

            def last_yz(i, carry):
                shears(i + 1, ROWS, side, (5,))
                return carry

            lax.fori_loop(0, depth, last_xy, 0)
            out_copy(3).start()
            arrive(2, step)
            lax.fori_loop(0, depth, last_rest, 0)
            for f in (0, 1, 2, 4):
                out_copy(f).start()
            edges(2, step)
            lax.fori_loop(0, depth, last_yz, 0)
            out_copy(5).start()

    w_out[...] = wbuf[...]
    for f in range(3):
        wait_sent(there, STEPS - 1, f)
        wait_sent(back, STEPS - 1, f)
    for f in range(3):
        v_copy(f).wait()
    for f in range(6):
        out_copy(f).wait()


def fused_body(
    n, ng, velocity, stress, pier_velocity, buoyancy, layer, lame_table, shear_table, relax_table,
    impedance, footprint, damp_inverse,
):
    depth, side, line = buoyancy.shape
    own = pier_velocity.shape[1]
    g = lax.axis_index("gy")
    w_all = lax.dynamic_update_slice(
        jnp.zeros((depth, LANES), jnp.float32), pier_velocity, (0, g * own)
    )
    imp = lax.dynamic_update_slice(
        jnp.zeros((ROWS, LANES), jnp.float32),
        jnp.broadcast_to(impedance[None, :], (ROWS, own)), (0, g * own)
    )
    f32 = jnp.float32
    hbm = pl.BlockSpec(memory_space=pl.ANY)
    vmem = pl.BlockSpec(memory_space=pltpu.VMEM)
    smem = pl.BlockSpec(memory_space=pltpu.SMEM)
    dma = pltpu.SemaphoreType.DMA
    tall = side + 2 * ROWS
    stage = 2 * depth + ROWS
    v, s, w = pl.pallas_call(
        functools.partial(fused, n, ng),
        out_shape=(
            jax.ShapeDtypeStruct(velocity.shape, f32),
            jax.ShapeDtypeStruct(stress.shape, f32),
            jax.ShapeDtypeStruct((depth, LANES), f32),
        ),
        in_specs=[hbm] * 3 + [smem] * 5 + [vmem] * 3,
        out_specs=(hbm, hbm, vmem),
        scratch_shapes=[
            pltpu.VMEM((3 * STEPS, depth + 2, tall, line), f32),
            pltpu.VMEM((6, depth + 2, tall, line), f32),
            pltpu.VMEM((depth, side, line), f32),
            pltpu.VMEM((3, depth + 2, ROWS, LANES), f32),
            pltpu.VMEM((3, depth, side, line), f32),
            pltpu.VMEM((3, n * depth, ROWS, LANES), f32),
            pltpu.VMEM((3, n * depth + 2, ROWS, LANES), f32),
            pltpu.VMEM((STEPS, ng, stage, LANES), f32),
            pltpu.VMEM((depth, LANES), f32),
            pltpu.VMEM((3, depth, line), f32),
            pltpu.VMEM((3, depth, line), f32),
            pltpu.VMEM((STEPS, 3, 2, depth + 2, line), f32),
            pltpu.VMEM((STEPS, 3, 2, depth + 2, line), f32),
            dma((10,)), dma((3,)), dma((3,)), dma((2,)), dma((2,)), dma((3,)), dma((3,)),
            dma((STEPS, 3, n)), dma((STEPS, 3, n)), dma((STEPS, 3, n)), dma((STEPS, 3, n)),
            dma((STEPS, ng)), dma((STEPS, ng)), dma((STEPS, 3, 2)), dma((STEPS, 3, 2)),
            dma((9,)),
        ],
        compiler_params=pltpu.CompilerParams(
            collective_id=0, has_side_effects=True, vmem_limit_bytes=60 * 1024 * 1024
        ),
    )(
        velocity, stress, buoyancy, layer, lame_table, shear_table, relax_table,
        footprint, w_all, imp, damp_inverse,
    )
    return v, s, lax.dynamic_slice(w, (0, g * own), (depth, own))


def whole_tiles(mesh, velocity, pier_velocity):
    n, ng = mesh.shape["gx"], mesh.shape["gy"]
    depth, side, line = velocity.shape[1] // n, velocity.shape[2] // ng, velocity.shape[3]
    return (
        line % LANES == 0
        and side % ROWS == 0
        and depth % ROWS == 0
        and (side // ROWS) * (line // LANES) == n
        and pier_velocity.shape[1] <= LANES
    )


def solution(mesh):
    placed = (
        P(None, "gx", "gy", None),
        P(None, "gx", "gy", None),
        P("gx", "gy"),
        P("gx", "gy", None),
        P("gx"),
        P(),
        P(),
        P(),
        P("gy"),
        P(),
        P(),
    )

    def run(*args):
        n, ng = mesh.shape["gx"], mesh.shape["gy"]
        if whole_tiles(mesh, args[0], args[2]):
            part = functools.partial(fused_body, n, ng)
        else:
            part = body
        return mapped(part)(*args)

    def mapped(part):
        return jax.shard_map(
            part,
            mesh=mesh,
            in_specs=placed,
            out_specs=(P(None, "gx", "gy", None), P(None, "gx", "gy", None), P("gx", "gy")),
            check_vma=False,
        )

    return run
```
